256 devices in a mesh: lon: 32 (over y_hi, z, core), ch: 8 (over x, y_lo).
Axes of the slice: x: 4, y: 4 (y_hi: 2, y_lo: 2; y = y_hi * 2 + y_lo), z: 8, core: 2. Of those that a mesh axis runs over, the one named last changes fastest.
Arguments:
- field: bfloat16 [256, 1536, 128], P('lon', 'ch'), may hold values from -6 to 6
- w_query: bfloat16 [1536, 1536], P('lon', 'ch'), may hold values from -0.15625 to 0.15625
- w_key: bfloat16 [1536, 1536], P('lon', 'ch'), may hold values from -0.15625 to 0.15625
- w_value: bfloat16 [1536, 1536], P('lon', 'ch'), may hold values from -0.15625 to 0.15625
- w_proj: bfloat16 [1536, 1536], P('ch', 'lon'), may hold values from -0.15625 to 0.15625
- w_up: bfloat16 [1536, 6144], P('lon', 'ch'), may hold values from -0.15625 to 0.15625
- w_down: bfloat16 [6144, 1536], P('ch', 'lon'), may hold values from -0.078125 to 0.078125
- logit_scale: float32 [24], P('ch'), may hold values from 10 to 100
- rel_bias: float32 [24, 15, 15], P('ch'), may hold values from 0 to 16
- gain_attn: float32 [1536], P('ch'), may hold values from 0.5 to 1.5
- gain_mlp: float32 [1536], P('ch'), may hold values from 0.5 to 1.5
Outputs:
- mixed: bfloat16 [256, 1536, 128], P('lon', 'ch')
The draws below stay inside these ranges and needn't reach their ends.
All inputs are finite; a program needn't handle non-finite values.
Results may differ from the reference program's by a relative error of at most 0.025.
Values may be sent and summed in bfloat16 or wider, within the bound.
A program may use at most 64 MiB of HBM per device.

```python
import math
import jax
import jax.numpy as jnp
import numpy as np
from jax import lax

D = 1536
HEADS = 24
FFN = 6144
WIN = 8
SHIFT = 4
LAT = 128
LON = 256
N_CH = 8


def steps_of(own_key, dims, shards, smallest, high):
    loudness = 1.0
    for dim, parts in shards:
        steps = jax.random.uniform(jax.random.fold_in(jax.random.fold_in(own_key, 6), dim), (parts,), jnp.float32, smallest / len(shards), high / len(shards))
        loudness = loudness * jnp.repeat(jnp.exp(steps), dims[dim] // parts).reshape((-1,) + (1,) * (len(dims) - 1 - dim))
    return loudness


def scatter_about(stream_key, dims, scale, reach, shards=(), dtype=jnp.bfloat16):
    drawn = scale * jax.random.normal(stream_key, dims, jnp.float32)
    if shards:
        drawn = drawn * steps_of(stream_key, dims, shards, -0.22, 0.18)
    return jnp.clip(drawn, -reach, reach).astype(dtype)


def setup_inputs(seed: int = 0) -> dict:
    splits = jax.random.split(jax.random.key(seed), 12)
    return {
        "field": scatter_about(splits[0], (LON, D, LAT), 1.0, 6.0, ((0, 32), (1, 8))),
        "w_query": scatter_about(splits[1], (D, D), D ** -0.5, 0.15625, ((0, 32), (1, 8))),
        "w_key": scatter_about(splits[2], (D, D), D ** -0.5, 0.15625, ((0, 32), (1, 8))),
        "w_value": scatter_about(splits[3], (D, D), D ** -0.5, 0.15625, ((0, 32), (1, 8))),
        "w_proj": scatter_about(splits[4], (D, D), D ** -0.5, 0.15625, ((0, 8), (1, 32))),
        "w_up": scatter_about(splits[5], (D, FFN), D ** -0.5, 0.15625, ((0, 32), (1, 8))),
        "w_down": scatter_about(splits[6], (FFN, D), FFN ** -0.5, 0.078125, ((0, 8), (1, 32))),
        "logit_scale": jnp.clip(jnp.exp(math.log(100.0) - 2.3025851 * jax.random.uniform(splits[7], (HEADS,), jnp.float32) ** steps_of(splits[7], (HEADS,), ((0, 8),), -0.2, 0.2)), 10.0, 100.0),
        "rel_bias": jnp.clip(16.0 * jax.random.uniform(splits[8], (HEADS, 2 * WIN - 1, 2 * WIN - 1), jnp.float32) ** steps_of(splits[8], (HEADS, 2 * WIN - 1, 2 * WIN - 1), ((0, 8),), -0.2, 0.2), 0.0, 16.0),
        "gain_attn": jnp.clip(1.0 + 0.1 * jax.random.normal(splits[9], (D,), jnp.float32), 0.5, 1.5),
        "gain_mlp": jnp.clip(1.0 + 0.1 * jax.random.normal(splits[10], (D,), jnp.float32), 0.5, 1.5),
    }


def to_windows(array, lat, cols, heads):
    size = array.shape[1] // heads
    array = array.reshape(lat // WIN, WIN, cols // WIN, WIN, heads, size)
    return array.transpose(0, 2, 4, 1, 3, 5).reshape(lat // WIN, cols // WIN, heads, WIN * WIN, size)

def from_windows(array, lat, cols):
    heads = array.shape[2]
    size = array.shape[4]
    array = array.reshape(lat // WIN, cols // WIN, heads, WIN, WIN, size)
    return array.transpose(0, 3, 1, 4, 2, 5).reshape(lat * cols, heads * size)

def unit_rows(array):
    array = array.astype(jnp.float32)
    return (array * lax.rsqrt(lax.optimization_barrier(jnp.sum(array * array, axis=-1, keepdims=True)) + 1e-06)).astype(jnp.bfloat16)

def bias_and_mask(table, lat):
    place = np.arange(WIN * WIN)
    row_of = place // WIN
    col_of = place % WIN
    delta_row = row_of[:, None] - row_of[None, :] + WIN - 1
    delta_col = col_of[:, None] - col_of[None, :] + WIN - 1
    bias = table[:, delta_row, delta_col]
    grid_row = jnp.arange(lat // WIN)[:, None] * WIN + jnp.asarray(row_of)[None, :]
    region = grid_row >= lat - SHIFT
    allowed = region[:, :, None] == region[:, None, :]
    mask = jnp.where(allowed, 0.0, -1000000000.0).astype(jnp.float32)
    return (bias, mask)

def window_attention(query, key_in, value, scale, table, lat, cols):
    heads = scale.shape[0]
    query_w = unit_rows(to_windows(query, lat, cols, heads)).astype(jnp.float32)
    key_w = unit_rows(to_windows(key_in, lat, cols, heads)).astype(jnp.float32)
    value_w = to_windows(value, lat, cols, heads).astype(jnp.float32)
    bias, mask = bias_and_mask(table, lat)
    scores = jnp.einsum('abhid,abhjd->abhij', query_w, key_w, precision=lax.Precision.HIGHEST)
    scores = scores * scale[:, None, None] + bias[None, None] + mask[:, None, None]
    top = lax.optimization_barrier(jnp.max(scores, axis=-1, keepdims=True))
    expo = jnp.exp(scores - top)
    probs = (expo / lax.optimization_barrier(jnp.sum(expo, axis=-1, keepdims=True))).astype(jnp.bfloat16)
    out = jnp.einsum('abhij,abhjd->abhid', probs.astype(jnp.float32), value_w, precision=lax.Precision.HIGHEST)
    return from_windows(out.astype(jnp.bfloat16), lat, cols)

def grouped(left, right):
    rows = left.shape[1] // N_CH
    total = jnp.zeros((left.shape[0], right.shape[1]), jnp.float32)
    for group in range(N_CH):
        part = jnp.dot(left[:, group * rows:(group + 1) * rows], right[group * rows:(group + 1) * rows], preferred_element_type=jnp.float32)
        total = total + lax.optimization_barrier(part.astype(jnp.bfloat16)).astype(jnp.float32)
    return total

def post_norm(resid, branch, gain):
    width = branch.shape[1]
    mean = lax.optimization_barrier(jnp.sum(branch, axis=1, keepdims=True)) / width
    var = lax.optimization_barrier(jnp.sum(branch * branch, axis=1, keepdims=True)) / width - mean * mean
    return (resid.astype(jnp.float32) + (branch - mean) * lax.rsqrt(var + 1e-05) * gain).astype(jnp.bfloat16)

def reference(field, w_query, w_key, w_value, w_proj, w_up, w_down, logit_scale, rel_bias, gain_attn, gain_mlp):
    grid = field.transpose(2, 0, 1)
    shifted = jnp.roll(grid, (-SHIFT, -SHIFT), (0, 1)).reshape(LAT * LON, D)
    query = jnp.dot(shifted, w_query, preferred_element_type=jnp.float32).astype(jnp.bfloat16)
    key_in = jnp.dot(shifted, w_key, preferred_element_type=jnp.float32).astype(jnp.bfloat16)
    value = jnp.dot(shifted, w_value, preferred_element_type=jnp.float32).astype(jnp.bfloat16)
    attended = window_attention(query, key_in, value, logit_scale, rel_bias, LAT, LON)
    after = post_norm(shifted, grouped(attended, w_proj), gain_attn)
    hidden = jax.nn.gelu(jnp.dot(after, w_up, preferred_element_type=jnp.float32), approximate=False).astype(jnp.bfloat16)
    block = post_norm(after, grouped(hidden, w_down), gain_mlp)
    rolled = jnp.roll(block.reshape(LAT, LON, D), (SHIFT, SHIFT), (0, 1))
    return rolled.transpose(1, 2, 0)
```

```python
import functools

import jax
import jax.numpy as jnp
from jax import lax
from jax.experimental import pallas as pl
from jax.experimental.pallas import tpu as pltpu
from jax.sharding import PartitionSpec as P

MESH = pl.DeviceIdType.MESH
BF = jnp.bfloat16
F32 = jnp.float32
D = 1536
NX, NY, NZ = 4, 4, 8
ROWS = 48
PACK = 768
TOK = 256
PART = 192
PIECE = 384
NCHUNK = 2
SEMS = 160


def nt(a, b):
    return lax.dot_general(a, b, (((1,), (1,)), ((), ())), preferred_element_type=F32)


def nn(a, b):
    return jnp.dot(a, b, preferred_element_type=F32)


def gelu(v):
    return 0.5 * v * (1.0 + lax.erf(v * 0.7071067811865476))


def kernel(
    blk, wp, aux, gain, out,
    gw, rin, xf, qs, at, pb, rp, af, hs, db, rd, ss, st, ga, ea, bias, ob,
    send, recv,
):
    lon = lax.axis_index("lon")
    ch = lax.axis_index("ch")
    x, yl = ch // 2, ch % 2
    core, z, yh = lon % 2, (lon // 2) % NZ, lon // (2 * NZ)
    y = yh * 2 + yl

    def at_x(dx):
        return (lon, ((x + dx) % NX) * 2 + yl)

    def at_z(dz):
        return ((yh * NZ + (z + dz) % NZ) * 2 + core, ch)

    def at_y(dy):
        yy = (y + dy) % NY
        return (((yy // 2) * NZ + z) * 2 + core, x * 2 + yy % 2)

    sibling = (lon + 1 - 2 * core, ch)
    partner = (lon, x * 2 + 1 - yl)

    def at_lon(dl, other):
        c = x * 2 + 1 - yl if other else ch
        return ((lon + dl) % 32, c)

    def peer(dx, other):
        c = 1 - yl if other else yl
        return (lon, ((x + dx) % NX) * 2 + c)

    peers = [(1, 0), (3, 0), (2, 0), (0, 1), (1, 1), (3, 1), (2, 1)]

    barrier = pltpu.get_barrier_semaphore()
    greeted = [peer(a, b) for a, b in peers]
    greeted += [at_z(1), at_z(-1), at_y(1), at_y(-1), sibling]
    greeted += [at_lon(1, 0), at_lon(1, 1), at_lon(-1, 0), at_lon(-1, 1)]
    for device in greeted:
        pl.semaphore_signal(barrier, inc=1, device_id=device, device_id_type=MESH)
    pl.semaphore_wait(barrier, len(greeted))

    started = []

    def push(src, dst, device):
        k = len(started)
        copy = pltpu.make_async_remote_copy(
            src_ref=src, dst_ref=dst, send_sem=send.at[k], recv_sem=recv.at[k],
            device_id=device, device_id_type=MESH,
        )
        copy.start()
        started.append(copy)
        return copy

    def wblock(t, yy, zz):
        return gw.at[t, yy % 2, yy // 2, zz % NZ, core]

    zc, yc, yr, dc = {}, {}, {}, {}

    def z_send(t, s):
        if s < 4:
            ref = wblock(t, y, z - s + 1 + NZ)
            zc[t, s, 1] = push(ref, ref, at_z(1))
            ref = wblock(t, y, z + s - 1)
            zc[t, s, -1] = push(ref, ref, at_z(-1))
        else:
            sign = -1 if t == 1 else 1
            ref = wblock(t, y, z - sign * 3 + NZ)
            zc[t, s, sign] = push(ref, ref, at_z(sign))

    def z_wait(t, s):
        for sign in (1, -1):
            if (t, s, sign) in zc:
                zc[t, s, sign].wait_recv()

    ORDER = [0, 1, -1, 2, -2, 3, -3, 4]

    def y_send_one(t, k):
        ref = wblock(t, y, z + ORDER[k] + NZ)
        yc[t, k, 1] = push(ref, ref, at_y(1))
        yc[t, k, -1] = push(ref, ref, at_y(-1))

    def y_relay_one(t, k):
        yc[t, k, 1].wait_recv()
        yc[t, k, -1].wait_recv()
        sign = 1 if k % 2 == 0 else -1
        ref = wblock(t, (y - sign + NY) % NY, z + ORDER[k] + NZ)
        yr[t, k] = push(ref, ref, at_y(sign))

    def group(t, yy, lo=0, size=NZ):
        yy = (yy + NY) % NY
        return gw.at[t, yy % 2, yy // 2, pl.ds(lo, size), core]

    def y_send_all(t):
        ref = group(t, y)
        yc[t, 1] = push(ref, ref, at_y(1))
        yc[t, -1] = push(ref, ref, at_y(-1))

    def y_relay_all(t):
        yc[t, 1].wait_recv()
        yc[t, -1].wait_recv()
        ref = group(t, y - 1, 0, 4)
        yr[t, 0] = push(ref, ref, at_y(1))
        ref = group(t, y + 1, 4, 4)
        yr[t, 1] = push(ref, ref, at_y(-1))

    def to_sibling(t, dy):
        ref = group(t, y + dy)
        dc[t, dy] = push(ref, ref, sibling)

    def sibling_wait(t):
        for dy in (0, 1, -1, 2):
            dc[t, dy].wait_recv()

    rows_mine = pl.ds(pl.multiple_of(yl * PART, PART), PART)
    ic = {}

    def input_send(g):
        for name, src, cg, device in (
            ("partner", blk.at[1 - yl, g, 1], 0, partner),
            ("west", blk.at[yl, g, 0], 1, at_lon(31, 0)),
            ("both", blk.at[1 - yl, g, 0], 1, at_lon(31, 1)),
        ):
            ic[g, name] = push(src, rin.at[g, cg, rows_mine], device)

    for t in range(3):
        gw[t, yl, yh, z, core] = wp[t]
    input_send(0)
    z_send(0, 1)
    input_send(1)
    y_send_one(0, 0)
    ea[yl] = aux[...]
    aux_copy = push(ea.at[yl], ea.at[yl], partner)
    lanes_mine = pl.ds(pl.multiple_of(x * PIECE, 128), PIECE)
    ga[yl, :, lanes_mine] = gain[...]
    gain_copies = [
        push(ga.at[yl, :, lanes_mine], ga.at[yl, :, lanes_mine], peer(a, b)) for a, b in peers
    ]

    xc, xr = {}, {}

    def x_send(g):
        for cp in ("partner", "west", "both"):
            ic[g, cp].wait_recv()
        rin[g, 0, rows_mine] = blk[yl, g, 1]
        for cg in range(2):
            piece = rin[g, cg].astype(F32).T.astype(BF)
            xf[g, pl.ds(cg * 128, 128), lanes_mine] = piece
        ref = xf.at[g, :, lanes_mine]
        xc[g, 1] = push(ref, ref, at_x(1))
        xc[g, -1] = push(ref, ref, at_x(3))

    def x_relay(g):
        for sign, half in ((1, 0), (-1, 1)):
            xc[g, sign].wait_recv()
            lanes = pl.ds(pl.multiple_of(((x + 4 - sign) % NX) * PIECE, 128), PIECE)
            ref = xf.at[g, pl.ds(half * 128, 128), lanes]
            xr[g, sign] = push(ref, ref, at_x(sign + 4))

    z_wait(0, 1)
    z_send(0, 2)
    x_send(0)
    y_send_one(0, 1)
    y_send_one(0, 2)
    z_wait(0, 2)
    z_send(0, 3)
    x_send(1)
    y_send_one(0, 3)
    y_send_one(0, 4)
    z_wait(0, 3)
    z_send(0, 4)
    y_send_one(0, 5)
    y_send_one(0, 6)
    z_send(1, 1)
    x_relay(0)
    y_relay_one(0, 0)
    z_wait(0, 4)
    y_send_one(0, 7)
    to_sibling(0, 0)
    z_wait(1, 1)
    z_send(1, 2)
    y_relay_one(0, 1)
    y_relay_one(0, 2)
    z_wait(1, 2)
    z_send(1, 3)
    y_relay_one(0, 3)
    x_relay(1)
    y_relay_one(0, 4)
    z_wait(1, 3)
    z_send(1, 4)
    y_relay_one(0, 5)
    y_relay_one(0, 6)
    y_relay_one(0, 7)
    to_sibling(0, 1)
    to_sibling(0, -1)
    z_send(2, 1)
    z_wait(1, 4)
    to_sibling(1, 0)
    y_send_all(1)
    z_wait(2, 1)
    z_send(2, 2)

    aux_copy.wait_recv()
    for part in range(2):
        for h in range(3):
            table = ea[part, h]
            for ci in range(8):
                bias[part, h, pl.ds(ci * 8, 8), :] = table[:, (7 - ci) * 8:(7 - ci) * 8 + 64]
    z_wait(2, 2)
    z_send(2, 3)
    for k in range(8):
        yr[0, k].wait_recv()
    to_sibling(0, 2)
    z_wait(2, 3)
    z_send(2, 4)
    sibling_wait(0)
    z_wait(2, 4)
    to_sibling(2, 0)

    row_i = lax.broadcasted_iota(jnp.int32, (64, 64), 0) % 8
    row_j = lax.broadcasted_iota(jnp.int32, (64, 64), 1) % 8
    poles = jnp.where((row_i >= 4) != (row_j >= 4), -1e9, 0.0).astype(F32)

    def unit(v):
        return (v * lax.rsqrt(jnp.sum(v * v, axis=-1, keepdims=True) + 1e-6)).astype(BF)

    pc = {}

    def attention(g):
        xr[g, 1].wait_recv()
        xr[g, -1].wait_recv()
        for part in range(2):
            for lo, size in ((0, 256), (256, 256), (512, 128)):
                w = gw[0, part, :, :, :, :, lo:lo + size].reshape(D, size)
                r = nn(xf[g], w).astype(BF).astype(F32)
                qs[part, :, :, lo:lo + size] = r.reshape(8, 32, size)

        def window(w, carry):
            lat = pl.ds(pl.multiple_of(w * 8, 8), 8)
            last = jnp.logical_and(yl == 1, w == 3) if g == NCHUNK - 1 else None
            for part in range(2):
                qkv = qs[part, :, lat, :].reshape(64, 640)
                heads = [jnp.zeros((64, 64), F32)]
                for h in range(3):
                    q = unit(qkv[:, h * 64:h * 64 + 64])
                    k = unit(qkv[:, 192 + h * 64:256 + h * 64])
                    v = qkv[:, 384 + h * 64:448 + h * 64].astype(BF)
                    s = nt(q, k) * ea[part, 3 + h, 0:1, 0:1] + bias[part, h]
                    if last is not None:
                        s = s + jnp.where(last, poles, 0.0)
                    e = jnp.exp(s - jnp.max(s, axis=-1, keepdims=True))
                    p = (e / jnp.sum(e, axis=-1, keepdims=True)).astype(BF)
                    heads.append(nn(p, v))
                o = jnp.concatenate(heads, axis=1)
                at[:, lat, part * 256:part * 256 + 256] = o.reshape(8, 8, 256)
            return carry

        lax.fori_loop(0, 4, window, 0)

        a = at[...].reshape(TOK, 512).astype(BF)

        def columns(n, carry):
            total = jnp.zeros((TOK, PIECE), F32)
            for part in range(2):
                w = gw[0, part, n // 2, pl.ds((n % 2) * 4, 4), :, :, 512:768].reshape(PIECE, 256)
                total = total + nt(a[:, part * 256:part * 256 + 256], w)
            lanes = pl.ds(pl.multiple_of(n * PIECE, 128), PIECE)
            pb[g, :, lanes] = total.astype(BF)
            return carry

        lax.fori_loop(0, 4, columns, 0)
        for slot, dx in ((0, 2), (1, 1), (2, 3)):
            rows = pl.ds(pl.multiple_of(((x + dx) % NX) * 64, 64), 64)
            pc[g, slot] = push(pb.at[g, rows], rp.at[g, slot], at_x(dx))

    ac, ar = {}, {}
    my_rows = pl.ds(pl.multiple_of(x * 64, 64), 64)

    def norm_one(g):
        for slot in range(3):
            pc[g, slot].wait_recv()
        v = pb[g, my_rows, :].astype(F32)
        for slot in range(3):
            v = v + rp[g, slot].astype(F32)
        mean = jnp.sum(v, axis=1, keepdims=True) * (1.0 / D)
        var = jnp.sum(v * v, axis=1, keepdims=True) * (1.0 / D) - mean * mean
        gains = ga[0, 0:1, :] + ga[1, 0:1, :]
        res = xf[g, my_rows, :].astype(F32)
        af[g, my_rows, :] = (res + (v - mean) * lax.rsqrt(var + 1e-5) * gains).astype(BF)
        ref = af.at[g, my_rows]
        ac[g, 1] = push(ref, ref, at_x(1))
        ac[g, -1] = push(ref, ref, at_x(3))

    def a_relay(g):
        for sign, half in ((1, 0), (-1, 1)):
            ac[g, sign].wait_recv()
            start = ((x + 4 - sign) % NX) * 64 + half * 32
            ref = af.at[g, pl.ds(pl.multiple_of(start, 32), 32)]
            ar[g, sign] = push(ref, ref, at_x(sign + 4))

    def up(g):
        ar[g, 1].wait_recv()
        ar[g, -1].wait_recv()

        def columns(n, carry):
            lo = pl.multiple_of((n % 3) * 256, 256)
            w = gw[1, n // 3, :, :, :, :, pl.ds(lo, 256)].reshape(D, 256)
            hs[:, pl.ds(pl.multiple_of(n * 256, 256), 256)] = gelu(nn(af[g], w)).astype(BF)
            return carry

        lax.fori_loop(0, 6, columns, 0)

    rc = {}

    def down(g):
        for slot, dx in ((0, 2), (1, 1), (2, 3), (3, 0)):
            xx = (x + dx) % NX
            total = jnp.zeros((PIECE, TOK), F32)
            for part in range(2):
                w = gw[2, part, xx // 2, pl.ds((xx % 2) * 4, 4)].reshape(PIECE, PACK)
                total = total + nt(w, hs[:, part * PACK:part * PACK + PACK])
            db[g, slot] = total.astype(BF)
            if slot < 3:
                rc[g, slot] = push(db.at[g, slot], rd.at[g, slot], at_x(dx))

    sc = {}

    def stats(g):
        for slot in range(3):
            rc[g, slot].wait_recv()
        v = db[g, 3].astype(F32)
        for slot in range(3):
            v = v + rd[g, slot].astype(F32)
        one = jnp.sum(v, axis=0, keepdims=True)
        two = jnp.sum(v * v, axis=0, keepdims=True)
        ss[g, 0:1, :] = one
        ss[g, 1:2, :] = two
        for slot, dx in ((0, 2), (1, 1), (2, 3)):
            sc[g, slot] = push(ss.at[g], st.at[g, slot], at_x(dx))
        return v

    oc = []

    def final(g, v):
        res = af[g, :, lanes_mine].astype(F32).T
        row = ga[0, 1:2, lanes_mine] + ga[1, 1:2, lanes_mine]
        col = jnp.broadcast_to(row, (128, PIECE)).T
        gains = jnp.concatenate([col, col], axis=1)
        for slot in range(3):
            sc[g, slot].wait_recv()
        tot = ss[g] + st[g, 0] + st[g, 1] + st[g, 2]
        mean = tot[0:1] * (1.0 / D)
        var = tot[1:2] * (1.0 / D) - mean * mean
        o = (res + (v - mean) * lax.rsqrt(var + 1e-5) * gains).astype(BF)
        for cg in range(2):
            ob[g, cg] = o[:, cg * 128:cg * 128 + 128].reshape(2, PART, 128)
        out[yl, g, 1] = ob[g, 0, yl]
        for src, half, device in (
            (ob.at[g, 0, 1 - yl], 1, partner),
            (ob.at[g, 1, yl], 0, at_lon(1, 0)),
            (ob.at[g, 1, 1 - yl], 0, at_lon(1, 1)),
        ):
            oc.append(push(src, out.at[yl, g, half], device))

    ss[...] = jnp.zeros_like(ss)
    attention(0)
    y_relay_all(1)
    to_sibling(1, 1)
    to_sibling(1, -1)
    y_send_all(2)
    attention(1)
    for cp in gain_copies:
        cp.wait_recv()
    norm_one(0)
    yr[1, 0].wait_recv()
    yr[1, 1].wait_recv()
    to_sibling(1, 2)
    y_relay_all(2)
    to_sibling(2, 1)
    to_sibling(2, -1)
    a_relay(0)
    norm_one(1)
    sibling_wait(1)
    up(0)
    a_relay(1)
    yr[2, 0].wait_recv()
    yr[2, 1].wait_recv()
    to_sibling(2, 2)
    sibling_wait(2)
    down(0)
    up(1)
    down(1)
    v0 = stats(0)
    final(0, v0)
    v1 = stats(1)
    final(1, v1)
    for cp in oc:
        cp.wait_recv()
    for cp in started:
        cp.wait_send()


def body(
    field, w_query, w_key, w_value, w_proj, w_up, w_down, logit_scale, rel_bias, gain_attn, gain_mlp
):
    rolled = jnp.roll(field, -4, axis=2).reshape(2, 4, PART, 2, 2, 32)
    blk = rolled.transpose(3, 4, 0, 2, 1, 5).reshape(2, 2, 2, PART, 128)
    wp = jnp.stack(
        [
            jnp.concatenate([w_query, w_key, w_value, w_proj.T], axis=1),
            w_up,
            w_down.T,
        ]
    )
    flipped = rel_bias[:, ::-1, ::-1]
    table = jnp.stack([flipped[:, 7 - r:15 - r, :] for r in range(8)], axis=1)
    table = jnp.pad(table.transpose(0, 1, 3, 2), ((0, 0), (0, 0), (0, 1), (0, 0)))
    aux = jnp.concatenate(
        [
            table.reshape(3, 8, 128),
            jnp.broadcast_to(logit_scale[:, None, None], (3, 8, 128)),
            jnp.zeros((2, 8, 128), F32),
        ]
    )
    second = lax.axis_index("ch") % 2
    both = jnp.stack([gain_attn, gain_mlp])
    both = jnp.concatenate(
        [jnp.where(second == 0, both, 0.0), jnp.where(second == 1, both, 0.0)], axis=1
    )
    gain = jnp.pad(both, ((0, 6), (0, 0)))
    vmem = pl.BlockSpec(memory_space=pltpu.VMEM)
    out = pl.pallas_call(
        kernel,
        out_shape=jax.ShapeDtypeStruct((2, 2, 2, PART, 128), BF),
        in_specs=[vmem] * 4,
        out_specs=vmem,
        scratch_shapes=[
            pltpu.VMEM((3, 2, 2, NZ, 2, ROWS, PACK), BF),
            pltpu.VMEM((2, 2, PIECE, 128), BF),
            pltpu.VMEM((2, TOK, D), BF),
            pltpu.VMEM((2, 8, 32, 640), F32),
            pltpu.VMEM((8, 32, 512), F32),
            pltpu.VMEM((2, TOK, D), BF),
            pltpu.VMEM((2, 3, 64, D), BF),
            pltpu.VMEM((2, TOK, D), BF),
            pltpu.VMEM((TOK, D), BF),
            pltpu.VMEM((2, 4, PIECE, TOK), BF),
            pltpu.VMEM((2, 3, PIECE, TOK), BF),
            pltpu.VMEM((2, 8, TOK), F32),
            pltpu.VMEM((2, 3, 8, TOK), F32),
            pltpu.VMEM((2, 8, D), F32),
            pltpu.VMEM((2, 8, 8, 128), F32),
            pltpu.VMEM((2, 3, 64, 64), F32),
            pltpu.VMEM((2, 2, 2, PART, 128), BF),
            pltpu.SemaphoreType.DMA((SEMS,)),
            pltpu.SemaphoreType.DMA((SEMS,)),
        ],
        compiler_params=pltpu.CompilerParams(
            collective_id=0, has_side_effects=True, vmem_limit_bytes=52 << 20
        ),
        name="block",
    )(blk, wp, aux, gain)
    mixed = out.reshape(2, 2, 2, PART, 4, 32).transpose(2, 4, 3, 0, 1, 5)
    return jnp.roll(mixed.reshape(8, PART, 128), 4, axis=2)


def solution(mesh):
    placed = (
        P("lon", "ch", None),
        P("lon", "ch"),
        P("lon", "ch"),
        P("lon", "ch"),
        P("ch", "lon"),
        P("lon", "ch"),
        P("ch", "lon"),
        P("ch"),
        P("ch", None, None),
        P("ch"),
        P("ch"),
    )
    return jax.shard_map(
        body, mesh=mesh, in_specs=placed, out_specs=P("lon", "ch", None), check_vma=False
    )
```

```python
import jax
import jax.numpy as jnp
from jax import lax
from jax.experimental import pallas as pl
from jax.experimental.pallas import tpu as pltpu
from jax.sharding import PartitionSpec as P

MESH = pl.DeviceIdType.MESH
BF = jnp.bfloat16
F32 = jnp.float32
D = 1536
NX, NY, NZ = 4, 4, 8
ROWS = 48
PACK = 768
TOK = 256
PART = 192
PIECE = 384
SEMS = 192


def nt(a, b):
    return lax.dot_general(a, b, (((1,), (1,)), ((), ())), preferred_element_type=F32)


def nn(a, b):
    return jnp.dot(a, b, preferred_element_type=F32)


def gelu(v):
    return 0.5 * v * (1.0 + lax.erf(v * 0.7071067811865476))


def by_column(v):
    v = v.reshape(4, 8, 8, v.shape[1])
    return jnp.concatenate([v[:, c].reshape(32, v.shape[3]) for c in range(8)], axis=0)


def kernel(
    field, w_query, w_key, w_value, w_proj, w_up, w_down, logit, rel, g_attn, g_mlp, out,
    fr, rq, rk, rv, rpj, sc, tb, rga, rgm,
    blk, gw, rin, xf, qn, kn, vn, at, pb, rl, rp, af, hs, db, rdl, rd, ss, st, ga, ea, bias, ob,
    load, send, recv,
):
    lon = lax.axis_index("lon")
    ch = lax.axis_index("ch")
    x, yl = ch // 2, ch % 2
    core, z, yh = lon % 2, (lon // 2) % NZ, lon // (2 * NZ)
    y = yh * 2 + yl
    way = 1 - 2 * core

    def at_x(dx):
        return (lon, ((x + dx + NX) % NX) * 2 + yl)

    def at_z(dz):
        return ((yh * NZ + (z + dz + NZ) % NZ) * 2 + core, ch)

    def at_y(dy):
        yy = (y + dy + NY) % NY
        return (((yy // 2) * NZ + z) * 2 + core, x * 2 + yy % 2)

    sibling = (lon + 1 - 2 * core, ch)
    partner = (lon, x * 2 + 1 - yl)

    def at_lon(dl, other):
        c = x * 2 + 1 - yl if other else ch
        return ((lon + dl + 32) % 32, c)

    def peer(dx, other):
        c = 1 - yl if other else yl
        return (lon, ((x + dx) % NX) * 2 + c)

    peers = [(1, 0), (3, 0), (2, 0), (0, 1), (1, 1), (3, 1), (2, 1)]

    loads = []
    for src, dst in (
        (field, fr), (w_query, rq), (w_key, rk), (w_value, rv), (w_proj, rpj),
        (w_up, gw.at[1, yl, yh, z, core]), (w_down, gw.at[2, yl, yh, z, core]),
        (logit, sc), (rel, tb), (g_attn, rga), (g_mlp, rgm),
    ):
        copy = pltpu.make_async_copy(src, dst, load.at[len(loads)])
        copy.start()
        loads.append(copy)

    barrier = pltpu.get_barrier_semaphore()
    greeted = [peer(a, b) for a, b in peers]
    greeted += [at_z(dz) for dz in (1, -1, 2, -2, 3, -3, 4)]
    greeted += [at_y(1), at_y(-1), at_y(2), sibling]
    greeted += [at_lon(1, 0), at_lon(1, 1), at_lon(-1, 0), at_lon(-1, 1)]
    for device in greeted:
        pl.semaphore_signal(barrier, inc=1, device_id=device, device_id_type=MESH)

    for copy in loads:
        copy.wait()

    lane = lax.broadcasted_iota(jnp.int32, (32, 128), 1) // 32

    def regroup(i, carry):
        rows = pl.ds(pl.multiple_of(i * 32, 32), 32)
        for half in range(2):
            cols = [fr[half * 4 + j, rows, :].astype(F32) for j in range(4)]
            for k in range(4):
                v = None
                for j in range(4):
                    moved = pltpu.roll(cols[j], (32 * (j - k) - 4) % 128, 1)
                    v = moved if v is None else jnp.where(lane == j, moved, v)
                blk[k // 2, k % 2, half, rows, :] = v.astype(BF)
        return carry

    lax.fori_loop(0, PART // 32, regroup, 0)
    q, k, v = (r[...].astype(F32) for r in (rq, rk, rv))
    p = rpj[...].astype(F32)
    gw[0, yl, yh, z, core] = jnp.concatenate(
        [
            q[:, :128], k[:, :128], v[:, :128], q[:, 128:], k[:, 128:],
            v[:, 128:], p[:, 128:], p[:, :128],
        ],
        axis=1,
    ).astype(BF)

    pl.semaphore_wait(barrier, len(greeted))

    started = []

    def push(src, dst, device):
        i = len(started)
        copy = pltpu.make_async_remote_copy(
            src_ref=src, dst_ref=dst, send_sem=send.at[i], recv_sem=recv.at[i],
            device_id=device, device_id_type=MESH,
        )
        copy.start()
        started.append(copy)
        return copy

    def share(ref, device):
        return push(ref, ref, device)

    UPPER, LOWER = pl.ds(0, 32), pl.ds(32, 16)
    zc, yc, yr, dc = {}, {}, {}, {}

    def wblock(t, yy, zz, rows=pl.ds(0, ROWS)):
        return gw.at[t, yy % 2, yy // 2, zz % NZ, core, rows]

    def ring_send(key, s, ref_of):
        if s < 4:
            zc[key, s, 1] = share(ref_of(z - s + 1 + NZ), at_z(1))
            zc[key, s, -1] = share(ref_of(z + s - 1), at_z(-1))
        else:
            zc[key, s, 0] = share(ref_of(z - way * 3 + NZ), at_z(way))

    def ring_wait(key, s):
        for sign in (1, -1, 0):
            if (key, s, sign) in zc:
                zc[key, s, sign].wait_recv()

    ORDER = [0, 1, -1, 2, -2, 3, -3, 4]

    def y_send_one(k):
        ref = wblock(0, y, z + ORDER[k] + NZ, UPPER)
        yc[k, 1] = share(ref, at_y(1))
        yc[k, -1] = share(ref, at_y(-1))

    def y_relay_one(k):
        yc[k, 1].wait_recv()
        yc[k, -1].wait_recv()
        sign = 1 if k % 2 == 0 else -1
        yr[k] = share(wblock(0, (y - sign + NY) % NY, z + ORDER[k] + NZ, UPPER), at_y(sign))

    def group(t, dy, zs=pl.ds(0, NZ), rows=pl.ds(0, ROWS)):
        yy = (y + dy + NY) % NY
        return gw.at[t, yy % 2, yy // 2, zs, core, rows]

    def upper(dz):
        return wblock(0, y, z + dz + NZ, UPPER)

    def lower(dz):
        return gw.at[0, :, :, (z + dz + NZ) % NZ, core, LOWER]

    def far_send(key, ref_of):
        for dz in (2, -2, 1, -1):
            zc[key, dz] = share(ref_of(0), at_z(dz))

    def far_relay(key, ref_of):
        far_wait(key, 2, -2)
        zc[key, 3] = share(ref_of(-2), at_z(1))
        zc[key, -3] = share(ref_of(2), at_z(-1))
        zc[key, 4] = share(ref_of(-2 * way), at_z(2 * way))

    def far_wait(key, *steps):
        for dz in steps:
            zc[key, dz].wait_recv()

    def y_send(*ks):
        for k in ks:
            y_send_one(k)

    def y_relay(*ks):
        for k in ks:
            y_relay_one(k)

    def lower_to_sibling(*steps):
        for dz in steps:
            to_sibling("A", lower(dz))

    HALVES = (pl.ds(0, 4), pl.ds(4, 4))

    def up_z_send(*steps):
        for dz in steps:
            zc["U", dz] = share(wblock(1, y, z), at_z(dz))

    def up_y_send():
        for dz in (1, -1, 2, -2, 3, -3, 4):
            zc["U", dz].wait_recv()
        for half in range(2):
            for sign in (1, -1):
                yc["U", half, sign] = share(group(1, 0, HALVES[half]), at_y(sign))

    def up_y_relay(half):
        yc["U", half, 1].wait_recv()
        yc["U", half, -1].wait_recv()
        sign = 1 - 2 * half
        yr["U", half] = share(group(1, -sign, HALVES[half]), at_y(sign))

    def down_y_send():
        for dy in (1, -1, 2):
            yc["D", dy] = share(wblock(2, y, z), at_y(dy))

    def down_block(part):
        return lambda zz: gw.at[2, part, :, zz % NZ, core]

    def down_z(step):
        if step == 1:
            for dy in (1, -1, 2):
                yc["D", dy].wait_recv()
        for part in range(2):
            if step > 1:
                ring_wait(("D", part), step - 1)
            if step < 5:
                ring_send(("D", part), step, down_block(part))
        here = ((0,), (1, -1), (2, -2), (3, -3), (4,))[step - 1]
        for dz in here:
            to_sibling("D", plane(2, dz))

    def to_sibling(key, ref):
        dc.setdefault(key, []).append(share(ref, sibling))

    def sibling_wait(key):
        for copy in dc[key]:
            copy.wait_recv()

    def plane(t, dz, rows=pl.ds(0, ROWS)):
        return gw.at[t, :, :, (z + dz + NZ) % NZ, core, rows]

    rows_mine = pl.ds(pl.multiple_of(yl * PART, PART), PART)
    lanes_mine = pl.ds(pl.multiple_of(x * PIECE, 128), PIECE)
    ic = {}

    def input_send(g):
        for name, src, cg, device in (
            ("partner", blk.at[1 - yl, g, 1], 0, partner),
            ("both", blk.at[1 - yl, g, 0], 1, at_lon(-1, 1)),
            ("west", blk.at[yl, g, 0], 1, at_lon(-1, 0)),
        ):
            ic[g, name] = push(src, rin.at[g, cg, rows_mine], device)

    xc, xr = {}, {}

    def x_send(g):
        rin[g, 0, rows_mine] = blk[yl, g, 1]
        for name in ("partner", "both", "west"):
            ic[g, name].wait_recv()
        for cg in range(2):
            piece = rin[g, cg].astype(F32).T.reshape(4, 4, 8, PIECE)
            for w in range(4):
                part = piece[:, w].reshape(32, PIECE).astype(BF)
                xf[g, pl.ds(w * 64 + cg * 32, 32), lanes_mine] = part
        ref = xf.at[g, :, lanes_mine]
        xc[g, 1] = share(ref, at_x(1))
        xc[g, -1] = share(ref, at_x(-1))

    def x_relay(g):
        for sign, half in ((1, 0), (-1, 1)):
            xc[g, sign].wait_recv()
            lanes = pl.ds(pl.multiple_of(((x + 4 - sign) % NX) * PIECE, 128), PIECE)
            xr[g, sign] = share(xf.at[g, pl.ds(half * 128, 128), lanes], at_x(sign))

    def tables():
        k_of = lax.broadcasted_iota(jnp.int32, (15, 128), 1) // 8
        a_of = (
            lax.broadcasted_iota(jnp.int32, (8, 128), 1) % 8
            - lax.broadcasted_iota(jnp.int32, (8, 128), 0)
            + 7
        )
        for h in range(3):
            t = tb[h]
            wide = jnp.zeros((15, 128), F32)
            for b in range(15):
                wide = jnp.where(k_of == b, t[:, b:b + 1], wide)
            e = jnp.zeros((8, 128), F32)
            for a in range(15):
                e = jnp.where(a_of == a, wide[a:a + 1, :], e)
            ea[yl, h] = e
            ea[yl, 3 + h] = jnp.broadcast_to(sc[0:1, h:h + 1], (8, 128))
        copies = [share(ea.at[yl], partner)]
        here = lax.broadcasted_iota(jnp.int32, (1, PIECE), 1) // PART == yl
        rows = [
            jnp.where(here, jnp.concatenate([r[...], r[...]], axis=1), 0.0) for r in (rga, rgm)
        ]
        ga[yl, :, lanes_mine] = jnp.concatenate(rows + [jnp.zeros((6, PIECE), F32)], axis=0)
        ref = ga.at[yl, :, lanes_mine]
        return copies + [share(ref, peer(a, b)) for a, b in peers]

    row_j = lax.broadcasted_iota(jnp.int32, (64, 128), 0) % 8
    row_i = lax.broadcasted_iota(jnp.int32, (64, 128), 1) % 8
    poles = jnp.where((row_i >= 4) != (row_j >= 4), -1e9, 0.0).astype(F32)
    low = lax.broadcasted_iota(jnp.int32, (64, 128), 1) < 64
    low_bf = jnp.where(low, 1.0, 0.0).astype(BF)
    high_bf = jnp.where(low, 0.0, 1.0).astype(BF)
    HEADS_OF = [((0, 0), (0, 1)), ((1, 0), (1, 1)), ((0, 2), (1, 2))]

    def biases():
        for pair, members in enumerate(HEADS_OF):
            t0, t1 = (ea[part, h] for part, h in members)
            for cj in range(8):
                lo = (7 - cj) * 8
                bias[pair, pl.ds(cj * 8, 8), :] = jnp.concatenate(
                    [t0[:, lo:lo + 64], t1[:, lo:lo + 64]], axis=1
                )

    def unit(v):
        n = v.shape[1]
        same = (
            lax.broadcasted_iota(jnp.int32, (n, n), 0) // 64
            == lax.broadcasted_iota(jnp.int32, (n, n), 1) // 64
        )
        ones = jnp.where(same, 1.0, 0.0).astype(BF)
        square = v * v
        head = square.astype(BF)
        rest = (square - head.astype(F32)).astype(BF)
        total = nn(head, ones) + nn(rest, ones)
        return v * lax.rsqrt(total + 1e-6)

    def qkv(g):
        xr[g, 1].wait_recv()
        xr[g, -1].wait_recv()
        thirds = []
        for part in range(2):

            def product(lo, size):
                w = gw[0, part, :, :, :, :, lo:lo + size].reshape(D, size)
                return nn(xf[g], w).astype(BF).astype(F32)

            r = unit(product(0, 256))
            qn[part] = r[:, :128].astype(BF)
            kn[part] = r[:, 128:].astype(BF)
            r = product(256, 256)
            vn[part] = r[:, :128].astype(BF)
            thirds.append((unit(r[:, 128:]), product(512, 128)))
        first = lax.broadcasted_iota(jnp.int32, (TOK, 128), 1) < 64
        (a0, v0), (a1, v1) = thirds
        qn[2] = jnp.where(first, a0, pltpu.roll(a1, 64, 1)).astype(BF)
        kn[2] = jnp.where(first, pltpu.roll(a0, 64, 1), a1).astype(BF)
        vn[2] = jnp.where(first, v0, pltpu.roll(v1, 64, 1)).astype(BF)

    def windows(g):
        def window(w, carry):
            rows = pl.ds(pl.multiple_of(w * 64, 64), 64)
            for pair, ((p0, h0), (p1, h1)) in enumerate(HEADS_OF):
                qq = qn[pair, rows]
                both = jnp.concatenate([qq * low_bf, qq * high_bf], axis=0)
                s = nt(kn[pair, rows], both)
                scale = jnp.where(low[0:1], ea[p0, 3 + h0, 0:1, :], ea[p1, 3 + h1, 0:1, :])
                s = s * scale + bias[pair]
                if g == 1:
                    s = s + jnp.where(jnp.logical_and(yl == 1, w == 3), poles, 0.0)
                e = jnp.exp(s - jnp.max(s, axis=0, keepdims=True))
                e = e * (1.0 / jnp.sum(e, axis=0, keepdims=True))
                o = nn(e.T.astype(BF), vn[pair, rows])
                o = jnp.where(low, o[:64], o[64:])
                if pair < 2:
                    at[pair, rows, 128:256] = o.astype(BF)
                else:
                    at[0, rows, 0:128] = jnp.where(low, 0.0, pltpu.roll(o, 64, 1)).astype(BF)
                    at[1, rows, 0:128] = jnp.where(low, 0.0, o).astype(BF)
            return carry

        for w in range(4):
            window(w, 0)

    def x_rows(dx):
        return pl.ds(pl.multiple_of(((x + dx + NX) % NX) * 64, 64), 64)

    LEFT, RIGHT = pl.ds(0, 768), pl.ds(768, 768)
    pc = {}

    def proj(g):
        def columns(n, carry):
            total = None
            for part in range(2):
                w = gw[0, part, n // 2, pl.ds((n % 2) * 4, 4), :, :, 512:768].reshape(PIECE, 256)
                term = nt(at[part], w)
                total = term if total is None else total + term
            pb[g, :, pl.ds(pl.multiple_of(n * PIECE, 128), PIECE)] = total.astype(BF)
            return carry

        lax.fori_loop(0, 4, columns, 0)
        pc[g, "l", 1] = push(pb.at[g, x_rows(2), LEFT], rl.at[g, 0], at_x(1))
        pc[g, "l", -1] = push(pb.at[g, x_rows(2), RIGHT], rl.at[g, 1], at_x(-1))
        pc[g, "n", 1] = push(pb.at[g, x_rows(1), RIGHT], rp.at[g, 0, :, RIGHT], at_x(1))
        pc[g, "n", -1] = push(pb.at[g, x_rows(-1), LEFT], rp.at[g, 1, :, LEFT], at_x(-1))

    def proj_relay(g):
        for slot, (sign, lanes) in enumerate(((1, LEFT), (-1, RIGHT))):
            pc[g, "l", sign].wait_recv()
            rows = x_rows(sign)
            v = pb[g, rows, lanes].astype(F32) + rl[g, slot].astype(F32)
            pb[g, rows, lanes] = v.astype(BF)
            pc[g, "s", sign] = push(pb.at[g, rows, lanes], rp.at[g, slot, :, lanes], at_x(sign))

    ac, ar = {}, {}

    def norm_one(g):
        for what in ("n", "s"):
            for sign in (1, -1):
                pc[g, what, sign].wait_recv()
        v = pb[g, x_rows(0), :].astype(F32) + rp[g, 0].astype(F32) + rp[g, 1].astype(F32)
        mean = jnp.sum(v, axis=1, keepdims=True) * (1.0 / D)
        var = jnp.sum(v * v, axis=1, keepdims=True) * (1.0 / D) - mean * mean
        gains = ga[0, 0:1, :] + ga[1, 0:1, :]
        res = xf[g, x_rows(0), :].astype(F32)
        af[g, x_rows(0), :] = (res + (v - mean) * lax.rsqrt(var + 1e-5) * gains).astype(BF)
        ref = af.at[g, x_rows(0)]
        ac[g, 1] = share(ref, at_x(1))
        ac[g, -1] = share(ref, at_x(-1))

    def a_relay(g):
        for sign, half in ((1, 0), (-1, 1)):
            ac[g, sign].wait_recv()
            start = ((x + 4 - sign) % NX) * 64 + half * 32
            ref = af.at[g, pl.ds(pl.multiple_of(start, 32), 32)]
            ar[g, sign] = share(ref, at_x(sign))

    def up(g):
        ar[g, 1].wait_recv()
        ar[g, -1].wait_recv()

        def columns(n, carry):
            lo = pl.multiple_of((n % 3) * 256, 256)
            w = gw[1, n // 3, :, :, :, :, pl.ds(lo, 256)].reshape(D, 256)
            v = by_column(gelu(nn(af[g], w))).astype(BF)
            hs[:, pl.ds(pl.multiple_of(n * 256, 256), 256)] = v
            return carry

        lax.fori_loop(0, 6, columns, 0)

    TOP, BOTTOM = pl.ds(0, PART), pl.ds(PART, PART)
    rc = {}

    def down(g):
        for slot, dx in ((0, 2), (1, 1), (2, 3), (3, 0)):
            xx = (x + dx) % NX
            total = None
            for part in range(2):
                w = gw[2, part, xx // 2, pl.ds((xx % 2) * 4, 4)].reshape(PIECE, PACK)
                term = nt(w, hs[:, part * PACK:part * PACK + PACK])
                total = term if total is None else total + term
            db[g, slot] = total.astype(BF)
            if slot == 0:
                rc[g, "l", 1] = push(db.at[g, 0, TOP], rdl.at[g, 0], at_x(1))
                rc[g, "l", -1] = push(db.at[g, 0, BOTTOM], rdl.at[g, 1], at_x(-1))
            elif slot == 1:
                rc[g, "n", 1] = push(db.at[g, 1, BOTTOM], rd.at[g, 0, BOTTOM], at_x(1))
            elif slot == 2:
                rc[g, "n", -1] = push(db.at[g, 2, TOP], rd.at[g, 1, TOP], at_x(-1))

    def down_relay(g):
        for slot, (sign, rows) in enumerate(((1, TOP), (-1, BOTTOM))):
            rc[g, "l", sign].wait_recv()
            v = db[g, slot + 1, rows].astype(F32) + rdl[g, slot].astype(F32)
            db[g, slot + 1, rows] = v.astype(BF)
            rc[g, "s", sign] = push(db.at[g, slot + 1, rows], rd.at[g, slot, rows], at_x(sign))

    tc = {}

    def stats(g):
        for what in ("n", "s"):
            for sign in (1, -1):
                rc[g, what, sign].wait_recv()
        v = db[g, 3].astype(F32) + rd[g, 0].astype(F32) + rd[g, 1].astype(F32)
        ss[g, 0:1, :] = jnp.sum(v, axis=0, keepdims=True)
        ss[g, 1:2, :] = jnp.sum(v * v, axis=0, keepdims=True)
        for slot, dx in ((0, 2), (1, 1), (2, 3)):
            tc[g, slot] = push(ss.at[g], st.at[g, slot], at_x(dx))
        return v

    oc = []

    def final(g, v):
        res = by_column(af[g, :, lanes_mine].astype(F32)).T
        row = ga[0, 1:2, lanes_mine] + ga[1, 1:2, lanes_mine]
        col = jnp.broadcast_to(row, (128, PIECE)).T
        gains = jnp.concatenate([col, col], axis=1)
        for slot in range(3):
            tc[g, slot].wait_recv()
        tot = ss[g] + st[g, 0] + st[g, 1] + st[g, 2]
        mean = tot[0:1] * (1.0 / D)
        var = tot[1:2] * (1.0 / D) - mean * mean
        o = (res + (v - mean) * lax.rsqrt(var + 1e-5) * gains).astype(BF)
        for cg in range(2):
            ob[g, cg] = o[:, cg * 128:cg * 128 + 128].reshape(2, PART, 128)
        out[yl, g, 1] = ob[g, 0, yl]
        for src, half, device in (
            (ob.at[g, 0, 1 - yl], 1, partner),
            (ob.at[g, 1, 1 - yl], 0, at_lon(1, 1)),
            (ob.at[g, 1, yl], 0, at_lon(1, 0)),
        ):
            oc.append(push(src, out.at[yl, g, half], device))

    input_send(0)
    far_send("upper", upper)
    for dy in (1, -1, 2):
        yc["first", dy] = share(wblock(0, y, z, LOWER), at_y(dy))
    y_send(0)
    ss[...] = jnp.zeros_like(ss)
    far_relay("upper", upper)
    for dy in (1, -1, 2):
        yc["first", dy].wait_recv()
    far_send("lower", lower)
    far_wait("upper", 1, -1)
    y_send(1, 2, 3, 4)
    lower_to_sibling(0)
    input_send(1)
    x_send(0)
    far_relay("lower", lower)
    lower_to_sibling(2, -2)
    far_wait("upper", 3, -3)
    y_send(5, 6)
    y_relay(0)
    far_wait("upper", 4)
    y_send(7)
    to_sibling("A", group(0, 0, rows=UPPER))
    x_relay(0)
    y_relay(1, 2, 3, 4)
    x_send(1)
    small = tables()
    far_wait("lower", 1, -1)
    lower_to_sibling(1, -1)
    y_relay(5, 6, 7)
    up_z_send(2, -2, 3, -3, 1, -1, 4)
    down_y_send()
    to_sibling("A", group(0, 1, rows=UPPER))
    to_sibling("A", group(0, -1, rows=UPPER))
    x_relay(1)
    far_wait("lower", 3, -3, 4)
    lower_to_sibling(3, -3, 4)
    for copy in small:
        copy.wait_recv()
    biases()
    for k in range(8):
        yr[k].wait_recv()
    to_sibling("A", group(0, 2, rows=UPPER))
    sibling_wait("A")
    qkv(0)
    down_z(1)
    windows(0)
    proj(0)
    up_y_send()
    to_sibling("U", group(1, 0))
    qkv(1)
    down_z(2)
    windows(1)
    proj_relay(0)
    proj(1)
    up_y_relay(0)
    norm_one(0)
    down_z(3)
    proj_relay(1)
    up_y_relay(1)
    to_sibling("U", group(1, 1))
    to_sibling("U", group(1, -1))
    a_relay(0)
    down_z(4)
    norm_one(1)
    yr["U", 0].wait_recv()
    yr["U", 1].wait_recv()
    to_sibling("U", group(1, 2))
    sibling_wait("U")
    up(0)
    a_relay(1)
    down_z(5)
    sibling_wait("D")
    down(0)
    up(1)
    down_relay(0)
    down(1)
    v0 = stats(0)
    down_relay(1)
    final(0, v0)
    v1 = stats(1)
    final(1, v1)
    for cp in oc:
        cp.wait_recv()
    for cp in started:
        cp.wait_send()


def body(
    field, w_query, w_key, w_value, w_proj, w_up, w_down, logit_scale, rel_bias, gain_attn, gain_mlp
):
    anywhere = pl.BlockSpec(memory_space=pl.ANY)
    out = pl.pallas_call(
        kernel,
        out_shape=jax.ShapeDtypeStruct((2, 2, 2, PART, 128), BF),
        in_specs=[anywhere] * 11,
        out_specs=pl.BlockSpec(memory_space=pltpu.VMEM),
        scratch_shapes=[
            pltpu.VMEM((8, PART, 128), BF),
            pltpu.VMEM((ROWS, PART), BF),
            pltpu.VMEM((ROWS, PART), BF),
            pltpu.VMEM((ROWS, PART), BF),
            pltpu.VMEM((ROWS, PART), BF),
            pltpu.VMEM((1, 3), F32),
            pltpu.VMEM((3, 15, 15), F32),
            pltpu.VMEM((1, PART), F32),
            pltpu.VMEM((1, PART), F32),
            pltpu.VMEM((2, 2, 2, PART, 128), BF),
            pltpu.VMEM((3, 2, 2, NZ, 2, ROWS, PACK), BF),
            pltpu.VMEM((2, 2, PIECE, 128), BF),
            pltpu.VMEM((2, TOK, D), BF),
            pltpu.VMEM((3, TOK, 128), BF),
            pltpu.VMEM((3, TOK, 128), BF),
            pltpu.VMEM((3, TOK, 128), BF),
            pltpu.VMEM((2, TOK, 256), BF),
            pltpu.VMEM((2, TOK, D), BF),
            pltpu.VMEM((2, 2, 64, 768), BF),
            pltpu.VMEM((2, 2, 64, D), BF),
            pltpu.VMEM((2, TOK, D), BF),
            pltpu.VMEM((TOK, D), BF),
            pltpu.VMEM((2, 4, PIECE, TOK), BF),
            pltpu.VMEM((2, 2, PART, TOK), BF),
            pltpu.VMEM((2, 2, PIECE, TOK), BF),
            pltpu.VMEM((2, 8, TOK), F32),
            pltpu.VMEM((2, 3, 8, TOK), F32),
            pltpu.VMEM((2, 8, D), F32),
            pltpu.VMEM((2, 8, 8, 128), F32),
            pltpu.VMEM((3, 64, 128), F32),
            pltpu.VMEM((2, 2, 2, PART, 128), BF),
            pltpu.SemaphoreType.DMA((11,)),
            pltpu.SemaphoreType.DMA((SEMS,)),
            pltpu.SemaphoreType.DMA((SEMS,)),
        ],
        compiler_params=pltpu.CompilerParams(
            collective_id=0, has_side_effects=True, vmem_limit_bytes=60 << 20
        ),
        name="block",
    )(
        field, w_query, w_key, w_value, w_proj.T, w_up, w_down.T,
        logit_scale.reshape(1, 3), rel_bias, gain_attn.reshape(1, PART), gain_mlp.reshape(1, PART),
    )
    mixed = out.reshape(2, 2, 2, PART, 4, 32).transpose(2, 4, 3, 0, 1, 5)
    return jnp.roll(mixed.reshape(8, PART, 128), 4, axis=2)


def solution(mesh):
    placed = (
        P("lon", "ch", None),
        P("lon", "ch"),
        P("lon", "ch"),
        P("lon", "ch"),
        P("ch", "lon"),
        P("lon", "ch"),
        P("ch", "lon"),
        P("ch"),
        P("ch", None, None),
        P("ch"),
        P("ch"),
    )
    return jax.shard_map(
        body, mesh=mesh, in_specs=placed, out_specs=P("lon", "ch", None), check_vma=False
    )
```

```python
import jax
import jax.numpy as jnp
from jax import lax
from jax.experimental import pallas as pl
from jax.experimental.pallas import tpu as pltpu
from jax.sharding import PartitionSpec as P

MESH = pl.DeviceIdType.MESH
BF = jnp.bfloat16
F32 = jnp.float32
D = 1536
NX, NY, NZ = 4, 4, 8
ROWS = 48
PACK = 768
TOK = 256
PART = 192
PIECE = 384
SEMS = 224


def nt(a, b):
    return lax.dot_general(a, b, (((1,), (1,)), ((), ())), preferred_element_type=F32)


def nn(a, b):
    return jnp.dot(a, b, preferred_element_type=F32)


def gelu(v):
    return 0.5 * v * (1.0 + lax.erf(v * 0.7071067811865476))


def by_column(v):
    v = v.reshape(4, 8, 8, v.shape[1])
    return jnp.concatenate([v[:, c].reshape(32, v.shape[3]) for c in range(8)], axis=0)


def kernel(
    field, w_query, w_key, w_value, w_proj, w_up, w_down, logit, rel, g_attn, g_mlp, out,
    fr, rq, rk, rv, rpj, sc, tb, rga, rgm,
    blk, gw, rin, xf, qn, kn, vn, third, at, pb, rl, rp, af, hs, db, rdl, rd, ss, st, ga, ea, bias, ob,
    load, send, recv,
):
    lon = lax.axis_index("lon")
    ch = lax.axis_index("ch")
    x, yl = ch // 2, ch % 2
    core, z, yh = lon % 2, (lon // 2) % NZ, lon // (2 * NZ)
    y = yh * 2 + yl
    way = 1 - 2 * core

    def at_x(dx):
        return (lon, ((x + dx + NX) % NX) * 2 + yl)

    def at_z(dz):
        return ((yh * NZ + (z + dz + NZ) % NZ) * 2 + core, ch)

    def at_y(dy):
        yy = (y + dy + NY) % NY
        return (((yy // 2) * NZ + z) * 2 + core, x * 2 + yy % 2)

    sibling = (lon + 1 - 2 * core, ch)
    partner = (lon, x * 2 + 1 - yl)

    def at_lon(dl, other):
        c = x * 2 + 1 - yl if other else ch
        return ((lon + dl + 32) % 32, c)

    def peer(dx, other):
        c = 1 - yl if other else yl
        return (lon, ((x + dx) % NX) * 2 + c)

    peers = [(1, 0), (3, 0), (2, 0), (0, 1), (1, 1), (3, 1), (2, 1)]

    loads = []
    for src, dst in (
        (field, fr), (w_query, rq), (w_key, rk), (w_value, rv), (w_proj, rpj),
        (w_up, gw.at[1, yl, yh, z, core]), (w_down, gw.at[2, yl, yh, z, core]),
        (logit, sc), (rel, tb), (g_attn, rga), (g_mlp, rgm),
    ):
        copy = pltpu.make_async_copy(src, dst, load.at[len(loads)])
        copy.start()
        loads.append(copy)

    barrier = pltpu.get_barrier_semaphore()
    greeted = [peer(a, b) for a, b in peers]
    greeted += [at_z(dz) for dz in (1, -1, 2, -2, 3, -3, 4)]
    greeted += [at_y(1), at_y(-1), at_y(2), sibling]
    greeted += [at_lon(1, 0), at_lon(1, 1), at_lon(-1, 0), at_lon(-1, 1)]
    for device in greeted:
        pl.semaphore_signal(barrier, inc=1, device_id=device, device_id_type=MESH)

    for copy in loads:
        copy.wait()

    lane = lax.broadcasted_iota(jnp.int32, (32, 128), 1) // 32

    def regroup(i, carry):
        rows = pl.ds(pl.multiple_of(i * 32, 32), 32)
        for half in range(2):
            cols = [fr[half * 4 + j, rows, :].astype(F32) for j in range(4)]
            for k in range(4):
                v = None
                for j in range(4):
                    moved = pltpu.roll(cols[j], (32 * (j - k) - 4) % 128, 1)
                    v = moved if v is None else jnp.where(lane == j, moved, v)
                blk[k // 2, k % 2, half, rows, :] = v.astype(BF)
        return carry

    lax.fori_loop(0, PART // 32, regroup, 0)
    q, k, v = (r[...].astype(F32) for r in (rq, rk, rv))
    p = rpj[...].astype(F32)
    gw[0, yl, yh, z, core] = jnp.concatenate(
        [
            q[:, :128], k[:, :128], v[:, :128], q[:, 128:], k[:, 128:],
            v[:, 128:], p[:, 128:], p[:, :128],
        ],
        axis=1,
    ).astype(BF)

    pl.semaphore_wait(barrier, len(greeted))

    started = []

    def push(src, dst, device):
        i = len(started)
        copy = pltpu.make_async_remote_copy(
            src_ref=src, dst_ref=dst, send_sem=send.at[i], recv_sem=recv.at[i],
            device_id=device, device_id_type=MESH,
        )
        copy.start()
        started.append(copy)
        return copy

    def share(ref, device):
        return push(ref, ref, device)

    UPPER, LOWER = pl.ds(0, 32), pl.ds(32, 16)
    zc, yc, yr, dc = {}, {}, {}, {}

    def wblock(t, yy, zz, rows=pl.ds(0, ROWS)):
        return gw.at[t, yy % 2, yy // 2, zz % NZ, core, rows]

    def ring_send(key, s, ref_of):
        if s < 4:
            zc[key, s, 1] = share(ref_of(z - s + 1 + NZ), at_z(1))
            zc[key, s, -1] = share(ref_of(z + s - 1), at_z(-1))
        else:
            zc[key, s, 0] = share(ref_of(z - way * 3 + NZ), at_z(way))

    def ring_wait(key, s):
        for sign in (1, -1, 0):
            if (key, s, sign) in zc:
                zc[key, s, sign].wait_recv()

    ORDER = [0, 1, -1, 2, -2, 3, -3, 4]

    def y_send_one(k):
        ref = wblock(0, y, z + ORDER[k] + NZ, UPPER)
        yc[k, 1] = share(ref, at_y(1))
        yc[k, -1] = share(ref, at_y(-1))

    def y_relay_one(k):
        yc[k, 1].wait_recv()
        yc[k, -1].wait_recv()
        sign = 1 if k % 2 == 0 else -1
        yr[k] = share(wblock(0, (y - sign + NY) % NY, z + ORDER[k] + NZ, UPPER), at_y(sign))

    def group(t, dy, zs=pl.ds(0, NZ), rows=pl.ds(0, ROWS)):
        yy = (y + dy + NY) % NY
        return gw.at[t, yy % 2, yy // 2, zs, core, rows]

    def upper(dz):
        return wblock(0, y, z + dz + NZ, UPPER)

    def lower(part):
        return lambda dz: gw.at[0, part, :, (z + dz + NZ) % NZ, core, LOWER]

    def far_send(key, ref_of, steps=(2, -2, 1, -1)):
        for dz in steps:
            zc[key, dz] = share(ref_of(0), at_z(dz))

    def far_relay(key, ref_of):
        far_wait(key, 2, -2)
        zc[key, 3] = share(ref_of(-2), at_z(1))
        zc[key, -3] = share(ref_of(2), at_z(-1))
        zc[key, 4] = share(ref_of(-2 * way), at_z(2 * way))

    def far_wait(key, *steps):
        for dz in steps:
            zc[key, dz].wait_recv()

    def y_send(*ks):
        for k in ks:
            y_send_one(k)

    def y_relay(*ks):
        for k in ks:
            y_relay_one(k)

    def lower_to_sibling(*steps):
        for dz in steps:
            to_sibling("A", gw.at[0, :, :, (z + dz + NZ) % NZ, core, LOWER])

    def lower_send():
        for steps in ((2, -2), (1, -1)):
            for part in range(2):
                far_send(("lower", part), lower(part), steps)

    def lower_wait(*steps):
        for part in range(2):
            far_wait(("lower", part), *steps)

    HALVES = (pl.ds(0, 4), pl.ds(4, 4))

    def up_block(dz):
        return wblock(1, y, z + dz + NZ)

    def up_y_send():
        far_wait("U", 1, -1, 3, -3, 4)
        for half in range(2):
            for sign in (1, -1):
                yc["U", half, sign] = share(group(1, 0, HALVES[half]), at_y(sign))

    def up_y_relay(half):
        yc["U", half, 1].wait_recv()
        yc["U", half, -1].wait_recv()
        sign = 1 - 2 * half
        yr["U", half] = share(group(1, -sign, HALVES[half]), at_y(sign))

    def down_y_send():
        for dy in (1, -1, 2):
            yc["D", dy] = share(wblock(2, y, z), at_y(dy))

    def down_block(part):
        return lambda zz: gw.at[2, part, :, zz % NZ, core]

    def down_z(step):
        if step == 1:
            for dy in (1, -1, 2):
                yc["D", dy].wait_recv()
        for part in range(2):
            if step > 1:
                ring_wait(("D", part), step - 1)
            if step < 5:
                ring_send(("D", part), step, down_block(part))
        here = ((0,), (1, -1), (2, -2), (3, -3), (4,))[step - 1]
        for dz in here:
            to_sibling("D", plane(2, dz))

    def to_sibling(key, ref):
        dc.setdefault(key, []).append(share(ref, sibling))

    def sibling_wait(key):
        for copy in dc[key]:
            copy.wait_recv()

    def plane(t, dz, rows=pl.ds(0, ROWS)):
        return gw.at[t, :, :, (z + dz + NZ) % NZ, core, rows]

    rows_mine = pl.ds(pl.multiple_of(yl * PART, PART), PART)
    lanes_mine = pl.ds(pl.multiple_of(x * PIECE, 128), PIECE)
    ic = {}

    def input_send(g):
        for name, src, cg, device in (
            ("partner", blk.at[1 - yl, g, 1], 0, partner),
            ("both", blk.at[1 - yl, g, 0], 1, at_lon(-1, 1)),
            ("west", blk.at[yl, g, 0], 1, at_lon(-1, 0)),
        ):
            ic[g, name] = push(src, rin.at[g, cg, rows_mine], device)

    xc, xr = {}, {}

    def x_send(g):
        rin[g, 0, rows_mine] = blk[yl, g, 1]
        for name in ("partner", "both", "west"):
            ic[g, name].wait_recv()
        for cg in range(2):
            piece = rin[g, cg].astype(F32).T.reshape(4, 4, 8, PIECE)
            for w in range(4):
                part = piece[:, w].reshape(32, PIECE).astype(BF)
                xf[g, pl.ds(w * 64 + cg * 32, 32), lanes_mine] = part
        for half in range(2):
            for sign in (1, -1):
                rows = pl.ds((half if sign == 1 else 1 - half) * 128, 128)
                xc[g, sign, half] = share(xf.at[g, rows, lanes_mine], at_x(sign))

    def x_relay(g):
        for sign, half in ((1, 0), (-1, 1)):
            xc[g, sign, 0].wait_recv()
            lanes = pl.ds(pl.multiple_of(((x + 4 - sign) % NX) * PIECE, 128), PIECE)
            xr[g, sign] = share(xf.at[g, pl.ds(half * 128, 128), lanes], at_x(sign))

    def tables():
        k_of = lax.broadcasted_iota(jnp.int32, (15, 128), 1) // 8
        a_of = (
            lax.broadcasted_iota(jnp.int32, (8, 128), 1) % 8
            - lax.broadcasted_iota(jnp.int32, (8, 128), 0)
            + 7
        )
        for h in range(3):
            t = tb[h]
            wide = jnp.zeros((15, 128), F32)
            for b in range(15):
                wide = jnp.where(k_of == b, t[:, b:b + 1], wide)
            e = jnp.zeros((8, 128), F32)
            for a in range(15):
                e = jnp.where(a_of == a, wide[a:a + 1, :], e)
            ea[yl, h] = e
            ea[yl, 3 + h] = jnp.broadcast_to(sc[0:1, h:h + 1], (8, 128))
        copies = [share(ea.at[yl], partner)]
        here = lax.broadcasted_iota(jnp.int32, (1, PIECE), 1) // PART == yl
        rows = [
            jnp.where(here, jnp.concatenate([r[...], r[...]], axis=1), 0.0) for r in (rga, rgm)
        ]
        ga[yl, :, lanes_mine] = jnp.concatenate(rows + [jnp.zeros((6, PIECE), F32)], axis=0)
        ref = ga.at[yl, :, lanes_mine]
        return copies + [share(ref, peer(a, b)) for a, b in peers]

    row_j = lax.broadcasted_iota(jnp.int32, (64, 128), 0) % 8
    row_i = lax.broadcasted_iota(jnp.int32, (64, 128), 1) % 8
    poles = jnp.where((row_i >= 4) != (row_j >= 4), -1e9, 0.0).astype(F32)
    low = lax.broadcasted_iota(jnp.int32, (64, 128), 1) < 64
    low_bf = jnp.where(low, 1.0, 0.0).astype(BF)
    high_bf = jnp.where(low, 0.0, 1.0).astype(BF)
    HEADS_OF = [((0, 0), (0, 1)), ((1, 0), (1, 1)), ((0, 2), (1, 2))]

    def biases():
        for pair, members in enumerate(HEADS_OF):
            t0, t1 = (ea[part, h] for part, h in members)
            for cj in range(8):
                lo = (7 - cj) * 8
                bias[pair, pl.ds(cj * 8, 8), :] = jnp.concatenate(
                    [t0[:, lo:lo + 64], t1[:, lo:lo + 64]], axis=1
                )

    def unit(v):
        n = v.shape[1]
        same = (
            lax.broadcasted_iota(jnp.int32, (n, n), 0) // 64
            == lax.broadcasted_iota(jnp.int32, (n, n), 1) // 64
        )
        ones = jnp.where(same, 1.0, 0.0).astype(BF)
        square = v * v
        head = square.astype(BF)
        rest = (square - head.astype(F32)).astype(BF)
        total = nn(head, ones) + nn(rest, ones)
        return v * lax.rsqrt(total + 1e-6)

    def whole(g):
        for sign in (1, -1):
            xc[g, sign, 1].wait_recv()
            xr[g, sign].wait_recv()

    def qkv(g, part):
        def product(lo, size):
            w = gw[0, part, :, :, :, :, lo:lo + size].reshape(D, size)
            return nn(xf[g], w).astype(BF).astype(F32)

        r = unit(product(0, 256))
        qn[g, part] = r[:, :128].astype(BF)
        kn[g, part] = r[:, 128:].astype(BF)
        r = product(256, 256)
        vn[g, part] = r[:, :128].astype(BF)
        third[g, part, 0] = unit(r[:, 128:])
        third[g, part, 1] = product(512, 128)

    def third_pair(g):
        first = lax.broadcasted_iota(jnp.int32, (TOK, 128), 1) < 64
        (a0, v0), (a1, v1) = ((third[g, part, 0], third[g, part, 1]) for part in range(2))
        qn[g, 2] = jnp.where(first, a0, pltpu.roll(a1, 64, 1)).astype(BF)
        kn[g, 2] = jnp.where(first, pltpu.roll(a0, 64, 1), a1).astype(BF)
        vn[g, 2] = jnp.where(first, v0, pltpu.roll(v1, 64, 1)).astype(BF)

    def windows(g):
        def window(w, carry):
            rows = pl.ds(pl.multiple_of(w * 64, 64), 64)
            for pair, ((p0, h0), (p1, h1)) in enumerate(HEADS_OF):
                qq = qn[g, pair, rows]
                both = jnp.concatenate([qq * low_bf, qq * high_bf], axis=0)
                s = nt(kn[g, pair, rows], both)
                scale = jnp.where(low[0:1], ea[p0, 3 + h0, 0:1, :], ea[p1, 3 + h1, 0:1, :])
                s = s * scale + bias[pair]
                if g == 1:
                    s = s + jnp.where(jnp.logical_and(yl == 1, w == 3), poles, 0.0)
                e = jnp.exp(s - jnp.max(s, axis=0, keepdims=True))
                e = e * (1.0 / jnp.sum(e, axis=0, keepdims=True))
                o = nn(e.T.astype(BF), vn[g, pair, rows])
                o = jnp.where(low, o[:64], o[64:])
                if pair < 2:
                    at[pair, rows, 128:256] = o.astype(BF)
                else:
                    at[0, rows, 0:128] = jnp.where(low, 0.0, pltpu.roll(o, 64, 1)).astype(BF)
                    at[1, rows, 0:128] = jnp.where(low, 0.0, o).astype(BF)
            return carry

        for w in range(4):
            window(w, 0)

    def x_rows(dx):
        return pl.ds(pl.multiple_of(((x + dx + NX) % NX) * 64, 64), 64)

    LEFT, RIGHT = pl.ds(0, 768), pl.ds(768, 768)
    pc = {}

    def proj(g):
        def columns(n, carry):
            total = None
            for part in range(2):
                w = gw[0, part, n // 2, pl.ds((n % 2) * 4, 4), :, :, 512:768].reshape(PIECE, 256)
                term = nt(at[part], w)
                total = term if total is None else total + term
            pb[g, :, pl.ds(pl.multiple_of(n * PIECE, 128), PIECE)] = total.astype(BF)
            return carry

        lax.fori_loop(0, 4, columns, 0)
        pc[g, "l", 1] = push(pb.at[g, x_rows(2), LEFT], rl.at[g, 0], at_x(1))
        pc[g, "l", -1] = push(pb.at[g, x_rows(2), RIGHT], rl.at[g, 1], at_x(-1))
        pc[g, "n", 1] = push(pb.at[g, x_rows(1), RIGHT], rp.at[g, 0, :, RIGHT], at_x(1))
        pc[g, "n", -1] = push(pb.at[g, x_rows(-1), LEFT], rp.at[g, 1, :, LEFT], at_x(-1))

    def proj_relay(g):
        for slot, (sign, lanes) in enumerate(((1, LEFT), (-1, RIGHT))):
            pc[g, "l", sign].wait_recv()
            rows = x_rows(sign)
            v = pb[g, rows, lanes].astype(F32) + rl[g, slot].astype(F32)
            pb[g, rows, lanes] = v.astype(BF)
            pc[g, "s", sign] = push(pb.at[g, rows, lanes], rp.at[g, slot, :, lanes], at_x(sign))

    ac, ar = {}, {}

    def norm_one(g):
        for what in ("n", "s"):
            for sign in (1, -1):
                pc[g, what, sign].wait_recv()
        v = pb[g, x_rows(0), :].astype(F32) + rp[g, 0].astype(F32) + rp[g, 1].astype(F32)
        mean = jnp.sum(v, axis=1, keepdims=True) * (1.0 / D)
        var = jnp.sum(v * v, axis=1, keepdims=True) * (1.0 / D) - mean * mean
        gains = ga[0, 0:1, :] + ga[1, 0:1, :]
        res = xf[g, x_rows(0), :].astype(F32)
        af[g, x_rows(0), :] = (res + (v - mean) * lax.rsqrt(var + 1e-5) * gains).astype(BF)
        for half in range(2):
            for sign in (1, -1):
                start = x * 64 + (half if sign == 1 else 1 - half) * 32
                ref = af.at[g, pl.ds(pl.multiple_of(start, 32), 32)]
                ac[g, sign, half] = share(ref, at_x(sign))

    def a_relay(g):
        for sign, half in ((1, 0), (-1, 1)):
            ac[g, sign, 0].wait_recv()
            start = ((x + 4 - sign) % NX) * 64 + half * 32
            ref = af.at[g, pl.ds(pl.multiple_of(start, 32), 32)]
            ar[g, sign] = share(ref, at_x(sign))

    def up(g):
        for sign in (1, -1):
            ac[g, sign, 1].wait_recv()
            ar[g, sign].wait_recv()

        def columns(n, carry):
            lo = pl.multiple_of((n % 3) * 256, 256)
            w = gw[1, n // 3, :, :, :, :, pl.ds(lo, 256)].reshape(D, 256)
            v = by_column(gelu(nn(af[g], w))).astype(BF)
            hs[:, pl.ds(pl.multiple_of(n * 256, 256), 256)] = v
            return carry

        lax.fori_loop(0, 6, columns, 0)

    TOP, BOTTOM = pl.ds(0, PART), pl.ds(PART, PART)
    rc = {}

    def half(c):
        return pl.ds(c * 128, 128)

    def down(g):
        for slot, dx in ((0, 2), (1, 1), (2, 3), (3, 0)):
            xx = (x + dx) % NX
            total = None
            for part in range(2):
                w = gw[2, part, xx // 2, pl.ds((xx % 2) * 4, 4)].reshape(PIECE, PACK)
                term = nt(w, hs[:, part * PACK:part * PACK + PACK])
                total = term if total is None else total + term
            db[g, slot] = total.astype(BF)
            for c in range(2):
                if slot == 0:
                    for to, (sign, rows) in enumerate(((1, TOP), (-1, BOTTOM))):
                        rc[g, c, "l", sign] = push(
                            db.at[g, 0, rows, half(c)], rdl.at[g, to, :, half(c)], at_x(sign)
                        )
                elif slot < 3:
                    sign, rows = ((1, BOTTOM), (-1, TOP))[slot - 1]
                    rc[g, c, "n", sign] = push(
                        db.at[g, slot, rows, half(c)],
                        rd.at[g, slot - 1, rows, half(c)],
                        at_x(sign),
                    )

    def down_relay(g, c):
        for slot, (sign, rows) in enumerate(((1, TOP), (-1, BOTTOM))):
            rc[g, c, "l", sign].wait_recv()
            v = db[g, slot + 1, rows, half(c)].astype(F32)
            v = v + rdl[g, slot, :, half(c)].astype(F32)
            db[g, slot + 1, rows, half(c)] = v.astype(BF)
            rc[g, c, "s", sign] = push(
                db.at[g, slot + 1, rows, half(c)], rd.at[g, slot, rows, half(c)], at_x(sign)
            )

    tc = {}

    def stats(g, c):
        for what in ("n", "s"):
            for sign in (1, -1):
                rc[g, c, what, sign].wait_recv()
        v = db[g, 3, :, half(c)].astype(F32)
        v = v + rd[g, 0, :, half(c)].astype(F32) + rd[g, 1, :, half(c)].astype(F32)
        ss[g, c, 0:1, :] = jnp.sum(v, axis=0, keepdims=True)
        ss[g, c, 1:2, :] = jnp.sum(v * v, axis=0, keepdims=True)
        for slot, dx in ((0, 2), (1, 1), (2, 3)):
            tc[g, c, slot] = push(ss.at[g, c], st.at[g, c, slot], at_x(dx))
        return v

    oc = []

    def residual(g):
        res = by_column(af[g, :, lanes_mine].astype(F32)).T
        row = ga[0, 1:2, lanes_mine] + ga[1, 1:2, lanes_mine]
        return res, jnp.broadcast_to(row, (128, PIECE)).T

    def final(g, c, v, res, gains):
        for slot in range(3):
            tc[g, c, slot].wait_recv()
        tot = ss[g, c] + st[g, c, 0] + st[g, c, 1] + st[g, c, 2]
        mean = tot[0:1] * (1.0 / D)
        var = tot[1:2] * (1.0 / D) - mean * mean
        o = res[:, c * 128:c * 128 + 128] + (v - mean) * lax.rsqrt(var + 1e-5) * gains
        ob[g, c] = o.astype(BF).reshape(2, PART, 128)
        if c == 0:
            out[yl, g, 1] = ob[g, 0, yl]
            oc.append(push(ob.at[g, 0, 1 - yl], out.at[yl, g, 1], partner))
        else:
            oc.append(push(ob.at[g, 1, 1 - yl], out.at[yl, g, 0], at_lon(1, 1)))
            oc.append(push(ob.at[g, 1, yl], out.at[yl, g, 0], at_lon(1, 0)))

    far_send("upper", upper)
    for dy in (1, -1, 2):
        yc["first", dy] = share(wblock(0, y, z, LOWER), at_y(dy))
    input_send(0)
    y_send(0)
    small = tables()
    ss[...] = jnp.zeros_like(ss)
    far_relay("upper", upper)
    for dy in (1, -1, 2):
        yc["first", dy].wait_recv()
    lower_send()
    input_send(1)
    far_wait("upper", 1, -1)
    y_send(1, 2, 3, 4)
    lower_to_sibling(0)
    x_send(0)
    far_wait("upper", 3, -3)
    y_send(5, 6)
    far_wait("upper", 4)
    y_send(7)
    y_relay(0)
    far_relay(("lower", 0), lower(0))
    far_relay(("lower", 1), lower(1))
    far_send("U", up_block)
    lower_to_sibling(2, -2)
    to_sibling("A", group(0, 0, rows=UPPER))
    x_relay(0)
    y_relay(1, 2, 3, 4)
    x_send(1)
    lower_wait(1, -1)
    lower_to_sibling(1, -1)
    y_relay(5, 6, 7)
    down_y_send()
    to_sibling("A", group(0, 1, rows=UPPER))
    to_sibling("A", group(0, -1, rows=UPPER))
    lower_wait(3, -3, 4)
    lower_to_sibling(3, -3, 4)
    x_relay(1)
    far_relay("U", up_block)
    for copy in small:
        copy.wait_recv()
    biases()
    for k in range(8):
        yr[k].wait_recv()
    to_sibling("B", group(0, 2, rows=UPPER))
    sibling_wait("A")
    whole(0)
    qkv(0, 1 - yl)
    down_z(1)
    whole(1)
    qkv(1, 1 - yl)
    sibling_wait("B")
    qkv(0, yl)
    third_pair(0)
    up_y_send()
    to_sibling("U", group(1, 0))
    windows(0)
    proj(0)
    qkv(1, yl)
    third_pair(1)
    down_z(2)
    windows(1)
    proj_relay(0)
    proj(1)
    up_y_relay(0)
    norm_one(0)
    down_z(3)
    proj_relay(1)
    up_y_relay(1)
    to_sibling("U", group(1, 1))
    to_sibling("U", group(1, -1))
    a_relay(0)
    yr["U", 0].wait_recv()
    yr["U", 1].wait_recv()
    to_sibling("U", group(1, 2))
    down_z(4)
    norm_one(1)
    sibling_wait("U")
    up(0)
    a_relay(1)
    down_z(5)
    sibling_wait("D")
    down(0)
    up(1)
    down_relay(0, 0)
    down_relay(0, 1)
    down(1)
    v0 = [stats(0, c) for c in range(2)]
    for c in range(2):
        down_relay(1, c)
    kept = residual(0)
    for c in range(2):
        final(0, c, v0[c], *kept)
    kept = residual(1)
    v1 = [stats(1, c) for c in range(2)]
    for c in range(2):
        final(1, c, v1[c], *kept)
    for cp in oc:
        cp.wait_recv()
    for cp in started:
        cp.wait_send()


def body(
    field, w_query, w_key, w_value, w_proj, w_up, w_down, logit_scale, rel_bias, gain_attn, gain_mlp
):
    anywhere = pl.BlockSpec(memory_space=pl.ANY)
    out = pl.pallas_call(
        kernel,
        out_shape=jax.ShapeDtypeStruct((2, 2, 2, PART, 128), BF),
        in_specs=[anywhere] * 11,
        out_specs=pl.BlockSpec(memory_space=pltpu.VMEM),
        scratch_shapes=[
            pltpu.VMEM((8, PART, 128), BF),
            pltpu.VMEM((ROWS, PART), BF),
            pltpu.VMEM((ROWS, PART), BF),
            pltpu.VMEM((ROWS, PART), BF),
            pltpu.VMEM((ROWS, PART), BF),
            pltpu.VMEM((1, 3), F32),
            pltpu.VMEM((3, 15, 15), F32),
            pltpu.VMEM((1, PART), F32),
            pltpu.VMEM((1, PART), F32),
            pltpu.VMEM((2, 2, 2, PART, 128), BF),
            pltpu.VMEM((3, 2, 2, NZ, 2, ROWS, PACK), BF),
            pltpu.VMEM((2, 2, PIECE, 128), BF),
            pltpu.VMEM((2, TOK, D), BF),
            pltpu.VMEM((2, 3, TOK, 128), BF),
            pltpu.VMEM((2, 3, TOK, 128), BF),
            pltpu.VMEM((2, 3, TOK, 128), BF),
            pltpu.VMEM((2, 2, 2, TOK, 128), F32),
            pltpu.VMEM((2, TOK, 256), BF),
            pltpu.VMEM((2, TOK, D), BF),
            pltpu.VMEM((2, 2, 64, 768), BF),
            pltpu.VMEM((2, 2, 64, D), BF),
            pltpu.VMEM((2, TOK, D), BF),
            pltpu.VMEM((TOK, D), BF),
            pltpu.VMEM((2, 4, PIECE, TOK), BF),
            pltpu.VMEM((2, 2, PART, TOK), BF),
            pltpu.VMEM((2, 2, PIECE, TOK), BF),
            pltpu.VMEM((2, 2, 8, 128), F32),
            pltpu.VMEM((2, 2, 3, 8, 128), F32),
            pltpu.VMEM((2, 8, D), F32),
            pltpu.VMEM((2, 8, 8, 128), F32),
            pltpu.VMEM((3, 64, 128), F32),
            pltpu.VMEM((2, 2, 2, PART, 128), BF),
            pltpu.SemaphoreType.DMA((11,)),
            pltpu.SemaphoreType.DMA((SEMS,)),
            pltpu.SemaphoreType.DMA((SEMS,)),
        ],
        compiler_params=pltpu.CompilerParams(
            collective_id=0, has_side_effects=True, vmem_limit_bytes=60 << 20
        ),
        name="block",
    )(
        field, w_query, w_key, w_value, w_proj.T, w_up, w_down.T,
        logit_scale.reshape(1, 3), rel_bias, gain_attn.reshape(1, PART), gain_mlp.reshape(1, PART),
    )
    mixed = out.reshape(2, 2, 2, PART, 4, 32).transpose(2, 4, 3, 0, 1, 5)
    return jnp.roll(mixed.reshape(8, PART, 128), 4, axis=2)


def solution(mesh):
    placed = (
        P("lon", "ch", None),
        P("lon", "ch"),
        P("lon", "ch"),
        P("lon", "ch"),
        P("ch", "lon"),
        P("lon", "ch"),
        P("ch", "lon"),
        P("ch"),
        P("ch", None, None),
        P("ch"),
        P("ch"),
    )
    return jax.shard_map(
        body, mesh=mesh, in_specs=placed, out_specs=P("lon", "ch", None), check_vma=False
    )
```

```python
import jax
import jax.numpy as jnp
from jax import lax
from jax.experimental import pallas as pl
from jax.experimental.pallas import tpu as pltpu
from jax.sharding import PartitionSpec as P

MESH = pl.DeviceIdType.MESH
BF = jnp.bfloat16
F32 = jnp.float32
D = 1536
NX, NY, NZ = 4, 4, 8
ROWS = 48
PACK = 768
TOK = 256
PART = 192
PIECE = 384
SEMS = 224


def nt(a, b):
    return lax.dot_general(a, b, (((1,), (1,)), ((), ())), preferred_element_type=F32)


def nn(a, b):
    return jnp.dot(a, b, preferred_element_type=F32)


def gelu(v):
    return 0.5 * v * (1.0 + lax.erf(v * 0.7071067811865476))


def by_column(v):
    v = v.reshape(4, 8, 8, v.shape[1])
    return jnp.concatenate([v[:, c].reshape(32, v.shape[3]) for c in range(8)], axis=0)


def kernel(
    field, w_query, w_key, w_value, w_proj, w_up, w_down, logit, rel, g_attn, g_mlp, out,
    fr, rq, rk, rv, rpj, sc, tb, rga, rgm,
    blk, gw, rin, xf, qn, kn, vn, third, at, pb, rl, rp, af, hs, db, rdl, rd, ss, st, ga, ea, bias, ob,
    load, send, recv,
):
    lon = lax.axis_index("lon")
    ch = lax.axis_index("ch")
    x, yl = ch // 2, ch % 2
    core, z, yh = lon % 2, (lon // 2) % NZ, lon // (2 * NZ)
    y = yh * 2 + yl
    way = 1 - 2 * core

    def at_x(dx):
        return (lon, ((x + dx + NX) % NX) * 2 + yl)

    def at_z(dz):
        return ((yh * NZ + (z + dz + NZ) % NZ) * 2 + core, ch)

    def at_y(dy):
        yy = (y + dy + NY) % NY
        return (((yy // 2) * NZ + z) * 2 + core, x * 2 + yy % 2)

    sibling = (lon + 1 - 2 * core, ch)
    partner = (lon, x * 2 + 1 - yl)

    def at_lon(dl, other):
        c = x * 2 + 1 - yl if other else ch
        return ((lon + dl + 32) % 32, c)

    def peer(dx, other):
        c = 1 - yl if other else yl
        return (lon, ((x + dx) % NX) * 2 + c)

    peers = [(1, 0), (3, 0), (2, 0), (0, 1), (1, 1), (3, 1), (2, 1)]

    loads = []
    for src, dst in (
        (field, fr), (w_query, rq), (w_key, rk), (w_value, rv), (w_proj, rpj),
        (w_up, gw.at[1, yl, yh, z, core]), (w_down, gw.at[2, yl, yh, z, core]),
        (logit, sc), (rel, tb), (g_attn, rga), (g_mlp, rgm),
    ):
        copy = pltpu.make_async_copy(src, dst, load.at[len(loads)])
        copy.start()
        loads.append(copy)

    barrier = pltpu.get_barrier_semaphore()
    greeted = [peer(a, b) for a, b in peers]
    greeted += [at_z(dz) for dz in (1, -1, 2, -2, 3, -3, 4)]
    greeted += [at_y(1), at_y(-1), at_y(2), sibling]
    greeted += [at_lon(1, 0), at_lon(1, 1), at_lon(-1, 0), at_lon(-1, 1)]
    for device in greeted:
        pl.semaphore_signal(barrier, inc=1, device_id=device, device_id_type=MESH)

    for copy in loads:
        copy.wait()

    lane = lax.broadcasted_iota(jnp.int32, (32, 128), 1) // 32

    def regroup(i, carry):
        rows = pl.ds(pl.multiple_of(i * 32, 32), 32)
        for half in range(2):
            cols = [fr[half * 4 + j, rows, :].astype(F32) for j in range(4)]
            for k in range(4):
                v = None
                for j in range(4):
                    moved = pltpu.roll(cols[j], (32 * (j - k) - 4) % 128, 1)
                    v = moved if v is None else jnp.where(lane == j, moved, v)
                blk[k // 2, k % 2, half, rows, :] = v.astype(BF)
        return carry

    lax.fori_loop(0, PART // 32, regroup, 0)
    q, k, v = (r[...].astype(F32) for r in (rq, rk, rv))
    p = rpj[...].astype(F32)
    gw[0, yl, yh, z, core] = jnp.concatenate(
        [
            q[:, :128], k[:, :128], v[:, :128], q[:, 128:], k[:, 128:],
            v[:, 128:], p[:, 128:], p[:, :128],
        ],
        axis=1,
    ).astype(BF)

    pl.semaphore_wait(barrier, len(greeted))

    started = []

    def push(src, dst, device):
        i = len(started)
        copy = pltpu.make_async_remote_copy(
            src_ref=src, dst_ref=dst, send_sem=send.at[i], recv_sem=recv.at[i],
            device_id=device, device_id_type=MESH,
        )
        copy.start()
        started.append(copy)
        return copy

    def share(ref, device):
        return push(ref, ref, device)

    UPPER, LOWER = pl.ds(0, 32), pl.ds(32, 16)
    zc, yc, yr, dc = {}, {}, {}, {}

    def wblock(t, yy, zz, rows=pl.ds(0, ROWS)):
        return gw.at[t, yy % 2, yy // 2, zz % NZ, core, rows]

    def ring_send(key, s, ref_of):
        if s < 4:
            zc[key, s, 1] = share(ref_of(z - s + 1 + NZ), at_z(1))
            zc[key, s, -1] = share(ref_of(z + s - 1), at_z(-1))
        else:
            zc[key, s, 0] = share(ref_of(z - way * 3 + NZ), at_z(way))

    def ring_wait(key, s):
        for sign in (1, -1, 0):
            if (key, s, sign) in zc:
                zc[key, s, sign].wait_recv()

    ORDER = [0, 1, -1, 2, -2, 3, -3, 4]

    def y_send_one(k):
        ref = wblock(0, y, z + ORDER[k] + NZ, UPPER)
        yc[k, 1] = share(ref, at_y(1))
        yc[k, -1] = share(ref, at_y(-1))

    def y_relay_one(k):
        yc[k, 1].wait_recv()
        yc[k, -1].wait_recv()
        sign = 1 if k % 2 == 0 else -1
        yr[k] = share(wblock(0, (y - sign + NY) % NY, z + ORDER[k] + NZ, UPPER), at_y(sign))

    def group(t, dy, zs=pl.ds(0, NZ), rows=pl.ds(0, ROWS)):
        yy = (y + dy + NY) % NY
        return gw.at[t, yy % 2, yy // 2, zs, core, rows]

    def upper(dz):
        return wblock(0, y, z + dz + NZ, UPPER)

    def lower(part):
        return lambda dz: gw.at[0, part, :, (z + dz + NZ) % NZ, core, LOWER]

    def far_send(key, ref_of, steps=(2, -2, 1, -1)):
        for dz in steps:
            zc[key, dz] = share(ref_of(0), at_z(dz))

    def far_relay(key, ref_of):
        far_wait(key, 2, -2)
        zc[key, 3] = share(ref_of(-2), at_z(1))
        zc[key, -3] = share(ref_of(2), at_z(-1))
        zc[key, 4] = share(ref_of(-2 * way), at_z(2 * way))

    def far_wait(key, *steps):
        for dz in steps:
            zc[key, dz].wait_recv()

    def y_send(*ks):
        for k in ks:
            y_send_one(k)

    def y_relay(*ks):
        for k in ks:
            y_relay_one(k)

    def lower_to_sibling(*steps):
        for dz in steps:
            to_sibling("A", gw.at[0, :, :, (z + dz + NZ) % NZ, core, LOWER])

    def lower_send():
        for steps in ((2, -2), (1, -1)):
            for part in range(2):
                far_send(("lower", part), lower(part), steps)

    def lower_wait(*steps):
        for part in range(2):
            far_wait(("lower", part), *steps)

    HALVES = (pl.ds(0, 4), pl.ds(4, 4))

    def up_block(dz):
        return wblock(1, y, z + dz + NZ)

    def up_y_send():
        far_wait("U", 1, -1, 3, -3, 4)
        for half in range(2):
            for sign in (1, -1):
                yc["U", half, sign] = share(group(1, 0, HALVES[half]), at_y(sign))

    def up_y_relay(half):
        yc["U", half, 1].wait_recv()
        yc["U", half, -1].wait_recv()
        sign = 1 - 2 * half
        yr["U", half] = share(group(1, -sign, HALVES[half]), at_y(sign))

    def down_y_send():
        for dy in (1, -1, 2):
            yc["D", dy] = share(wblock(2, y, z), at_y(dy))

    def down_block(part):
        return lambda zz: gw.at[2, part, :, zz % NZ, core]

    def down_z(step):
        if step == 1:
            for dy in (1, -1, 2):
                yc["D", dy].wait_recv()
        for part in range(2):
            if step > 1:
                ring_wait(("D", part), step - 1)
            if step < 5:
                ring_send(("D", part), step, down_block(part))
        here = ((0,), (1, -1), (2, -2), (3, -3), (4,))[step - 1]
        for dz in here:
            to_sibling("D", plane(2, dz))

    def to_sibling(key, ref):
        dc.setdefault(key, []).append(share(ref, sibling))

    def sibling_wait(key):
        for copy in dc[key]:
            copy.wait_recv()

    def plane(t, dz, rows=pl.ds(0, ROWS)):
        return gw.at[t, :, :, (z + dz + NZ) % NZ, core, rows]

    rows_mine = pl.ds(pl.multiple_of(yl * PART, PART), PART)
    lanes_mine = pl.ds(pl.multiple_of(x * PIECE, 128), PIECE)
    ic = {}

    def input_send(g):
        for name, src, cg, device in (
            ("partner", blk.at[1 - yl, g, 1], 0, partner),
            ("both", blk.at[1 - yl, g, 0], 1, at_lon(-1, 1)),
            ("west", blk.at[yl, g, 0], 1, at_lon(-1, 0)),
        ):
            ic[g, name] = push(src, rin.at[g, cg, rows_mine], device)

    xc, xr = {}, {}

    def x_send(g):
        rin[g, 0, rows_mine] = blk[yl, g, 1]
        for name in ("partner", "both", "west"):
            ic[g, name].wait_recv()
        for cg in range(2):
            piece = rin[g, cg].astype(F32).T.reshape(4, 4, 8, PIECE)
            for w in range(4):
                part = piece[:, w].reshape(32, PIECE).astype(BF)
                xf[g, pl.ds(w * 64 + cg * 32, 32), lanes_mine] = part
        for half in range(2):
            for sign in (1, -1):
                rows = pl.ds((half if sign == 1 else 1 - half) * 128, 128)
                xc[g, sign, half] = share(xf.at[g, rows, lanes_mine], at_x(sign))

    def x_relay(g):
        for sign, half in ((1, 0), (-1, 1)):
            xc[g, sign, 0].wait_recv()
            lanes = pl.ds(pl.multiple_of(((x + 4 - sign) % NX) * PIECE, 128), PIECE)
            xr[g, sign] = share(xf.at[g, pl.ds(half * 128, 128), lanes], at_x(sign))

    def tables():
        k_of = lax.broadcasted_iota(jnp.int32, (15, 128), 1) // 8
        a_of = (
            lax.broadcasted_iota(jnp.int32, (8, 128), 1) % 8
            - lax.broadcasted_iota(jnp.int32, (8, 128), 0)
            + 7
        )
        for h in range(3):
            t = tb[h]
            wide = jnp.zeros((15, 128), F32)
            for b in range(15):
                wide = jnp.where(k_of == b, t[:, b:b + 1], wide)
            e = jnp.zeros((8, 128), F32)
            for a in range(15):
                e = jnp.where(a_of == a, wide[a:a + 1, :], e)
            ea[yl, h] = e
            ea[yl, 3 + h] = jnp.broadcast_to(sc[0:1, h:h + 1], (8, 128))
        copies = [share(ea.at[yl], partner)]
        here = lax.broadcasted_iota(jnp.int32, (1, PIECE), 1) // PART == yl
        rows = [
            jnp.where(here, jnp.concatenate([r[...], r[...]], axis=1), 0.0) for r in (rga, rgm)
        ]
        ga[yl, :, lanes_mine] = jnp.concatenate(rows + [jnp.zeros((6, PIECE), F32)], axis=0)
        ref = ga.at[yl, :, lanes_mine]
        return copies + [share(ref, peer(a, b)) for a, b in peers]

    row_j = lax.broadcasted_iota(jnp.int32, (64, 128), 0) % 8
    row_i = lax.broadcasted_iota(jnp.int32, (64, 128), 1) % 8
    poles = jnp.where((row_i >= 4) != (row_j >= 4), -1e9, 0.0).astype(F32)
    low = lax.broadcasted_iota(jnp.int32, (64, 128), 1) < 64
    low_bf = jnp.where(low, 1.0, 0.0).astype(BF)
    high_bf = jnp.where(low, 0.0, 1.0).astype(BF)
    HEADS_OF = [((0, 0), (0, 1)), ((1, 0), (1, 1)), ((0, 2), (1, 2))]

    def biases():
        for pair, members in enumerate(HEADS_OF):
            t0, t1 = (ea[part, h] for part, h in members)
            for cj in range(8):
                lo = (7 - cj) * 8
                bias[pair, pl.ds(cj * 8, 8), :] = jnp.concatenate(
                    [t0[:, lo:lo + 64], t1[:, lo:lo + 64]], axis=1
                )

    def unit(v):
        n = v.shape[1]
        same = (
            lax.broadcasted_iota(jnp.int32, (n, n), 0) // 64
            == lax.broadcasted_iota(jnp.int32, (n, n), 1) // 64
        )
        ones = jnp.where(same, 1.0, 0.0).astype(BF)
        square = v * v
        head = square.astype(BF)
        rest = (square - head.astype(F32)).astype(BF)
        total = nn(head, ones) + nn(rest, ones)
        return v * lax.rsqrt(total + 1e-6)

    def whole(g):
        for sign in (1, -1):
            xc[g, sign, 1].wait_recv()
            xr[g, sign].wait_recv()

    def qkv(g, part):
        def product(lo, size):
            w = gw[0, part, :, :, :, :, lo:lo + size].reshape(D, size)
            return nn(xf[g], w).astype(BF).astype(F32)

        r = unit(product(0, 256))
        qn[g, part] = r[:, :128].astype(BF)
        kn[g, part] = r[:, 128:].astype(BF)
        r = product(256, 256)
        vn[g, part] = r[:, :128].astype(BF)
        third[g, part, 0] = unit(r[:, 128:])
        third[g, part, 1] = product(512, 128)

    def third_pair(g):
        first = lax.broadcasted_iota(jnp.int32, (TOK, 128), 1) < 64
        (a0, v0), (a1, v1) = ((third[g, part, 0], third[g, part, 1]) for part in range(2))
        qn[g, 2] = jnp.where(first, a0, pltpu.roll(a1, 64, 1)).astype(BF)
        kn[g, 2] = jnp.where(first, pltpu.roll(a0, 64, 1), a1).astype(BF)
        vn[g, 2] = jnp.where(first, v0, pltpu.roll(v1, 64, 1)).astype(BF)

    def windows(g):
        def window(w):
            rows = pl.ds(w * 64, 64)
            for pair, ((p0, h0), (p1, h1)) in enumerate(HEADS_OF):
                qq = qn[g, pair, rows]
                both = jnp.concatenate([qq * low_bf, qq * high_bf], axis=0)
                s = nt(kn[g, pair, rows], both)
                scale = jnp.where(low[0:1], ea[p0, 3 + h0, 0:1, :], ea[p1, 3 + h1, 0:1, :])
                s = s * scale + bias[pair]
                if g == 1 and w == 3:
                    s = s + jnp.where(yl == 1, poles, 0.0)
                e = jnp.exp(s - jnp.max(s, axis=0, keepdims=True))
                e = e * (1.0 / jnp.sum(e, axis=0, keepdims=True))
                o = nn(e.T.astype(BF), vn[g, pair, rows])
                o = jnp.where(low, o[:64], o[64:])
                if pair < 2:
                    at[pair, rows, 128:256] = o.astype(BF)
                else:
                    at[0, rows, 0:128] = jnp.where(low, 0.0, pltpu.roll(o, 64, 1)).astype(BF)
                    at[1, rows, 0:128] = jnp.where(low, 0.0, o).astype(BF)

        for w in range(4):
            window(w)

    def x_rows(dx):
        return pl.ds(pl.multiple_of(((x + dx + NX) % NX) * 64, 64), 64)

    LEFT, RIGHT = pl.ds(0, 768), pl.ds(768, 768)
    pc = {}

    def proj(g):
        def columns(n):
            total = None
            for part in range(2):
                w = gw[0, part, n // 2, pl.ds((n % 2) * 4, 4), :, :, 512:768].reshape(PIECE, 256)
                term = nt(at[part], w)
                total = term if total is None else total + term
            pb[g, :, pl.ds(n * PIECE, PIECE)] = total.astype(BF)

        for n in range(4):
            columns(n)
        pc[g, "l", 1] = push(pb.at[g, x_rows(2), LEFT], rl.at[g, 0], at_x(1))
        pc[g, "l", -1] = push(pb.at[g, x_rows(2), RIGHT], rl.at[g, 1], at_x(-1))
        pc[g, "n", 1] = push(pb.at[g, x_rows(1), RIGHT], rp.at[g, 0, :, RIGHT], at_x(1))
        pc[g, "n", -1] = push(pb.at[g, x_rows(-1), LEFT], rp.at[g, 1, :, LEFT], at_x(-1))

    def proj_relay(g):
        for slot, (sign, lanes) in enumerate(((1, LEFT), (-1, RIGHT))):
            pc[g, "l", sign].wait_recv()
            rows = x_rows(sign)
            v = pb[g, rows, lanes].astype(F32) + rl[g, slot].astype(F32)
            pb[g, rows, lanes] = v.astype(BF)
            pc[g, "s", sign] = push(pb.at[g, rows, lanes], rp.at[g, slot, :, lanes], at_x(sign))

    ac, ar = {}, {}

    def norm_one(g):
        for what in ("n", "s"):
            for sign in (1, -1):
                pc[g, what, sign].wait_recv()
        v = pb[g, x_rows(0), :].astype(F32) + rp[g, 0].astype(F32) + rp[g, 1].astype(F32)
        mean = jnp.sum(v, axis=1, keepdims=True) * (1.0 / D)
        var = jnp.sum(v * v, axis=1, keepdims=True) * (1.0 / D) - mean * mean
        gains = ga[0, 0:1, :] + ga[1, 0:1, :]
        res = xf[g, x_rows(0), :].astype(F32)
        af[g, x_rows(0), :] = (res + (v - mean) * lax.rsqrt(var + 1e-5) * gains).astype(BF)
        for half in range(2):
            for sign in (1, -1):
                start = x * 64 + (half if sign == 1 else 1 - half) * 32
                ref = af.at[g, pl.ds(pl.multiple_of(start, 32), 32)]
                ac[g, sign, half] = share(ref, at_x(sign))

    def a_relay(g):
        for sign, half in ((1, 0), (-1, 1)):
            ac[g, sign, 0].wait_recv()
            start = ((x + 4 - sign) % NX) * 64 + half * 32
            ref = af.at[g, pl.ds(pl.multiple_of(start, 32), 32)]
            ar[g, sign] = share(ref, at_x(sign))

    def up(g):
        for sign in (1, -1):
            ac[g, sign, 1].wait_recv()
            ar[g, sign].wait_recv()

        def columns(n):
            w = gw[1, n // 3, :, :, :, :, pl.ds((n % 3) * 256, 256)].reshape(D, 256)
            hs[:, pl.ds(n * 256, 256)] = by_column(gelu(nn(af[g], w))).astype(BF)

        for n in range(6):
            columns(n)

    TOP, BOTTOM = pl.ds(0, PART), pl.ds(PART, PART)
    rc = {}

    def half(c):
        return pl.ds(c * 128, 128)

    def down(g):
        for slot, dx in ((0, 2), (1, 1), (2, 3), (3, 0)):
            xx = (x + dx) % NX
            total = None
            for part in range(2):
                w = gw[2, part, xx // 2, pl.ds((xx % 2) * 4, 4)].reshape(PIECE, PACK)
                term = nt(w, hs[:, part * PACK:part * PACK + PACK])
                total = term if total is None else total + term
            db[g, slot] = total.astype(BF)
            for c in range(2):
                if slot == 0:
                    for to, (sign, rows) in enumerate(((1, TOP), (-1, BOTTOM))):
                        rc[g, c, "l", sign] = push(
                            db.at[g, 0, rows, half(c)], rdl.at[g, to, :, half(c)], at_x(sign)
                        )
                elif slot < 3:
                    sign, rows = ((1, BOTTOM), (-1, TOP))[slot - 1]
                    rc[g, c, "n", sign] = push(
                        db.at[g, slot, rows, half(c)],
                        rd.at[g, slot - 1, rows, half(c)],
                        at_x(sign),
                    )

    def down_relay(g, c):
        for slot, (sign, rows) in enumerate(((1, TOP), (-1, BOTTOM))):
            rc[g, c, "l", sign].wait_recv()
            v = db[g, slot + 1, rows, half(c)].astype(F32)
            v = v + rdl[g, slot, :, half(c)].astype(F32)
            db[g, slot + 1, rows, half(c)] = v.astype(BF)
            rc[g, c, "s", sign] = push(
                db.at[g, slot + 1, rows, half(c)], rd.at[g, slot, rows, half(c)], at_x(sign)
            )

    tc = {}

    def stats(g, c):
        for what in ("n", "s"):
            for sign in (1, -1):
                rc[g, c, what, sign].wait_recv()
        v = db[g, 3, :, half(c)].astype(F32)
        v = v + rd[g, 0, :, half(c)].astype(F32) + rd[g, 1, :, half(c)].astype(F32)
        ss[g, c, 0:1, :] = jnp.sum(v, axis=0, keepdims=True)
        ss[g, c, 1:2, :] = jnp.sum(v * v, axis=0, keepdims=True)
        for slot, dx in ((0, 2), (1, 1), (2, 3)):
            tc[g, c, slot] = push(ss.at[g, c], st.at[g, c, slot], at_x(dx))
        return v

    oc = []

    def residual(g):
        res = by_column(af[g, :, lanes_mine].astype(F32)).T
        row = ga[0, 1:2, lanes_mine] + ga[1, 1:2, lanes_mine]
        return res, jnp.broadcast_to(row, (128, PIECE)).T

    def final(g, c, v, res, gains):
        for slot in range(3):
            tc[g, c, slot].wait_recv()
        tot = ss[g, c] + st[g, c, 0] + st[g, c, 1] + st[g, c, 2]
        mean = tot[0:1] * (1.0 / D)
        var = tot[1:2] * (1.0 / D) - mean * mean
        o = res[:, c * 128:c * 128 + 128] + (v - mean) * lax.rsqrt(var + 1e-5) * gains
        ob[g, c] = o.astype(BF).reshape(2, PART, 128)
        if c == 0:
            out[yl, g, 1] = ob[g, 0, yl]
            oc.append(push(ob.at[g, 0, 1 - yl], out.at[yl, g, 1], partner))
        else:
            oc.append(push(ob.at[g, 1, 1 - yl], out.at[yl, g, 0], at_lon(1, 1)))
            oc.append(push(ob.at[g, 1, yl], out.at[yl, g, 0], at_lon(1, 0)))

    far_send("upper", upper)
    for dy in (1, -1, 2):
        yc["first", dy] = share(wblock(0, y, z, LOWER), at_y(dy))
    input_send(0)
    y_send(0)
    ss[...] = jnp.zeros_like(ss)
    far_relay("upper", upper)
    for dy in (1, -1, 2):
        yc["first", dy].wait_recv()
    lower_send()
    input_send(1)
    far_wait("upper", 1, -1)
    y_send(1, 2, 3, 4)
    lower_to_sibling(0)
    x_send(0)
    far_wait("upper", 3, -3)
    y_send(5, 6)
    far_wait("upper", 4)
    y_send(7)
    y_relay(0)
    far_relay(("lower", 0), lower(0))
    far_relay(("lower", 1), lower(1))
    far_send("U", up_block)
    lower_to_sibling(2, -2)
    to_sibling("A", group(0, 0, rows=UPPER))
    x_relay(0)
    y_relay(1, 2, 3, 4)
    x_send(1)
    lower_wait(1, -1)
    lower_to_sibling(1, -1)
    y_relay(5, 6, 7)
    small = tables()
    down_y_send()
    to_sibling("A", group(0, 1, rows=UPPER))
    to_sibling("A", group(0, -1, rows=UPPER))
    lower_wait(3, -3, 4)
    lower_to_sibling(3, -3, 4)
    x_relay(1)
    far_relay("U", up_block)
    for k in range(8):
        yr[k].wait_recv()
    to_sibling("B", group(0, 2, rows=UPPER))
    sibling_wait("A")
    whole(0)
    qkv(0, 1 - yl)
    down_z(1)
    whole(1)
    qkv(1, 1 - yl)
    sibling_wait("B")
    qkv(0, yl)
    third_pair(0)
    up_y_send()
    to_sibling("U", group(1, 0))
    for copy in small:
        copy.wait_recv()
    biases()
    windows(0)
    proj(0)
    qkv(1, yl)
    third_pair(1)
    down_z(2)
    windows(1)
    proj_relay(0)
    proj(1)
    up_y_relay(0)
    norm_one(0)
    down_z(3)
    proj_relay(1)
    up_y_relay(1)
    to_sibling("U", group(1, 1))
    to_sibling("U", group(1, -1))
    a_relay(0)
    yr["U", 0].wait_recv()
    yr["U", 1].wait_recv()
    to_sibling("U", group(1, 2))
    down_z(4)
    norm_one(1)
    sibling_wait("U")
    up(0)
    a_relay(1)
    down_z(5)
    sibling_wait("D")
    down(0)
    up(1)
    down_relay(0, 0)
    down_relay(0, 1)
    down(1)
    v0 = [stats(0, c) for c in range(2)]
    for c in range(2):
        down_relay(1, c)
    kept = residual(0)
    for c in range(2):
        final(0, c, v0[c], *kept)
    kept = residual(1)
    v1 = [stats(1, c) for c in range(2)]
    for c in range(2):
        final(1, c, v1[c], *kept)
    for cp in oc:
        cp.wait_recv()
    for cp in started:
        cp.wait_send()


def body(
    field, w_query, w_key, w_value, w_proj, w_up, w_down, logit_scale, rel_bias, gain_attn, gain_mlp
):
    anywhere = pl.BlockSpec(memory_space=pl.ANY)
    out = pl.pallas_call(
        kernel,
        out_shape=jax.ShapeDtypeStruct((2, 2, 2, PART, 128), BF),
        in_specs=[anywhere] * 11,
        out_specs=pl.BlockSpec(memory_space=pltpu.VMEM),
        scratch_shapes=[
            pltpu.VMEM((8, PART, 128), BF),
            pltpu.VMEM((ROWS, PART), BF),
            pltpu.VMEM((ROWS, PART), BF),
            pltpu.VMEM((ROWS, PART), BF),
            pltpu.VMEM((ROWS, PART), BF),
            pltpu.VMEM((1, 3), F32),
            pltpu.VMEM((3, 15, 15), F32),
            pltpu.VMEM((1, PART), F32),
            pltpu.VMEM((1, PART), F32),
            pltpu.VMEM((2, 2, 2, PART, 128), BF),
            pltpu.VMEM((3, 2, 2, NZ, 2, ROWS, PACK), BF),
            pltpu.VMEM((2, 2, PIECE, 128), BF),
            pltpu.VMEM((2, TOK, D), BF),
            pltpu.VMEM((2, 3, TOK, 128), BF),
            pltpu.VMEM((2, 3, TOK, 128), BF),
            pltpu.VMEM((2, 3, TOK, 128), BF),
            pltpu.VMEM((2, 2, 2, TOK, 128), F32),
            pltpu.VMEM((2, TOK, 256), BF),
            pltpu.VMEM((2, TOK, D), BF),
            pltpu.VMEM((2, 2, 64, 768), BF),
            pltpu.VMEM((2, 2, 64, D), BF),
            pltpu.VMEM((2, TOK, D), BF),
            pltpu.VMEM((TOK, D), BF),
            pltpu.VMEM((2, 4, PIECE, TOK), BF),
            pltpu.VMEM((2, 2, PART, TOK), BF),
            pltpu.VMEM((2, 2, PIECE, TOK), BF),
            pltpu.VMEM((2, 2, 8, 128), F32),
            pltpu.VMEM((2, 2, 3, 8, 128), F32),
            pltpu.VMEM((2, 8, D), F32),
            pltpu.VMEM((2, 8, 8, 128), F32),
            pltpu.VMEM((3, 64, 128), F32),
            pltpu.VMEM((2, 2, 2, PART, 128), BF),
            pltpu.SemaphoreType.DMA((11,)),
            pltpu.SemaphoreType.DMA((SEMS,)),
            pltpu.SemaphoreType.DMA((SEMS,)),
        ],
        compiler_params=pltpu.CompilerParams(
            collective_id=0, has_side_effects=True, vmem_limit_bytes=60 << 20
        ),
        name="block",
    )(
        field, w_query, w_key, w_value, w_proj.T, w_up, w_down.T,
        logit_scale.reshape(1, 3), rel_bias, gain_attn.reshape(1, PART), gain_mlp.reshape(1, PART),
    )
    mixed = out.reshape(2, 2, 2, PART, 4, 32).transpose(2, 4, 3, 0, 1, 5)
    return jnp.roll(mixed.reshape(8, PART, 128), 4, axis=2)


def solution(mesh):
    placed = (
        P("lon", "ch", None),
        P("lon", "ch"),
        P("lon", "ch"),
        P("lon", "ch"),
        P("ch", "lon"),
        P("lon", "ch"),
        P("ch", "lon"),
        P("ch"),
        P("ch", None, None),
        P("ch"),
        P("ch"),
    )
    return jax.shard_map(
        body, mesh=mesh, in_specs=placed, out_specs=P("lon", "ch", None), check_vma=False
    )
```

```python
import jax
import jax.numpy as jnp
from jax import lax
from jax.experimental import pallas as pl
from jax.experimental.pallas import tpu as pltpu
from jax.sharding import PartitionSpec as P

MESH = pl.DeviceIdType.MESH
BF = jnp.bfloat16
F32 = jnp.float32
D = 1536
NX, NY, NZ = 4, 4, 8
ROWS = 48
PACK = 768
TOK = 256
PART = 192
PIECE = 384
SEMS = 240


def nt(a, b):
    return lax.dot_general(a, b, (((1,), (1,)), ((), ())), preferred_element_type=F32)


def nn(a, b):
    return jnp.dot(a, b, preferred_element_type=F32)


def gelu(v):
    return 0.5 * v * (1.0 + lax.erf(v * 0.7071067811865476))


def by_column(v):
    v = v.reshape(4, 8, 8, v.shape[1])
    return jnp.concatenate([v[:, c].reshape(32, v.shape[3]) for c in range(8)], axis=0)


def kernel(
    field, w_query, w_key, w_value, w_proj, w_up, w_down, logit, rel, g_attn, g_mlp, out,
    fr, rq, rk, rv, rpj, sc, tb, rga, rgm,
    blk, gw, rin, xf, qn, kn, vn, third, at, pb, rl, rp, af, hs, db, rdl, rd, ss, st, ga, ea, bias, ob,
    load, send, recv,
):
    lon = lax.axis_index("lon")
    ch = lax.axis_index("ch")
    x, yl = ch // 2, ch % 2
    core, z, yh = lon % 2, (lon // 2) % NZ, lon // (2 * NZ)
    y = yh * 2 + yl
    way = 1 - 2 * core

    def at_x(dx):
        return (lon, ((x + dx + NX) % NX) * 2 + yl)

    def at_z(dz):
        return ((yh * NZ + (z + dz + NZ) % NZ) * 2 + core, ch)

    def at_y(dy):
        yy = (y + dy + NY) % NY
        return (((yy // 2) * NZ + z) * 2 + core, x * 2 + yy % 2)

    sibling = (lon + 1 - 2 * core, ch)
    partner = (lon, x * 2 + 1 - yl)

    def at_lon(dl, other):
        c = x * 2 + 1 - yl if other else ch
        return ((lon + dl + 32) % 32, c)

    def peer(dx, other):
        c = 1 - yl if other else yl
        return (lon, ((x + dx) % NX) * 2 + c)

    peers = [(1, 0), (3, 0), (2, 0), (0, 1), (1, 1), (3, 1), (2, 1)]

    loads = []
    for src, dst in (
        (field, fr), (w_query, rq), (w_key, rk), (w_value, rv), (w_proj, rpj),
        (w_up, gw.at[1, yl, yh, z, core]), (w_down, gw.at[2, yl, yh, z, core]),
        (logit, sc), (rel, tb), (g_attn, rga), (g_mlp, rgm),
    ):
        copy = pltpu.make_async_copy(src, dst, load.at[len(loads)])
        copy.start()
        loads.append(copy)

    barrier = pltpu.get_barrier_semaphore()
    greeted = [peer(a, b) for a, b in peers]
    greeted += [at_z(dz) for dz in (1, -1, 2, -2, 3, -3, 4)]
    greeted += [at_y(1), at_y(-1), at_y(2), sibling]
    greeted += [at_lon(1, 0), at_lon(1, 1), at_lon(-1, 0), at_lon(-1, 1)]
    for device in greeted:
        pl.semaphore_signal(barrier, inc=1, device_id=device, device_id_type=MESH)

    for copy in loads:
        copy.wait()

    lane = lax.broadcasted_iota(jnp.int32, (32, 128), 1) // 32

    def regroup(i, carry):
        rows = pl.ds(pl.multiple_of(i * 32, 32), 32)
        for half in range(2):
            cols = [fr[half * 4 + j, rows, :].astype(F32) for j in range(4)]
            for k in range(4):
                v = None
                for j in range(4):
                    moved = pltpu.roll(cols[j], (32 * (j - k) - 4) % 128, 1)
                    v = moved if v is None else jnp.where(lane == j, moved, v)
                blk[k // 2, k % 2, half, rows, :] = v.astype(BF)
        return carry

    lax.fori_loop(0, PART // 32, regroup, 0)
    q, k, v = (r[...].astype(F32) for r in (rq, rk, rv))
    p = rpj[...].astype(F32)
    gw[0, yl, yh, z, core] = jnp.concatenate(
        [
            q[:, :128], k[:, :128], v[:, :128], q[:, 128:], k[:, 128:],
            v[:, 128:], p[:, 128:], p[:, :128],
        ],
        axis=1,
    ).astype(BF)

    pl.semaphore_wait(barrier, len(greeted))

    started = []

    def push(src, dst, device):
        i = len(started)
        copy = pltpu.make_async_remote_copy(
            src_ref=src, dst_ref=dst, send_sem=send.at[i], recv_sem=recv.at[i],
            device_id=device, device_id_type=MESH,
        )
        copy.start()
        started.append(copy)
        return copy

    def share(ref, device):
        return push(ref, ref, device)

    UPPER, LOWER = pl.ds(0, 32), pl.ds(32, 16)
    zc, yc, yr, dc = {}, {}, {}, {}

    def wblock(t, yy, zz, rows=pl.ds(0, ROWS)):
        return gw.at[t, yy % 2, yy // 2, zz % NZ, core, rows]

    def ring_send(key, s, ref_of):
        if s < 4:
            zc[key, s, 1] = share(ref_of(z - s + 1 + NZ), at_z(1))
            zc[key, s, -1] = share(ref_of(z + s - 1), at_z(-1))
        else:
            zc[key, s, 0] = share(ref_of(z - way * 3 + NZ), at_z(way))

    def ring_wait(key, s):
        for sign in (1, -1, 0):
            if (key, s, sign) in zc:
                zc[key, s, sign].wait_recv()

    ORDER = [0, 1, -1, 2, -2, 3, -3, 4]

    def y_send_one(k, t, rows):
        ref = wblock(t, y, z + ORDER[k] + NZ, rows)
        yc[t, k, 1] = share(ref, at_y(1))
        yc[t, k, -1] = share(ref, at_y(-1))

    def y_relay_one(k, t, rows):
        yc[t, k, 1].wait_recv()
        yc[t, k, -1].wait_recv()
        sign = 1 if k % 2 == 0 else -1
        yr[t, k] = share(wblock(t, (y - sign + NY) % NY, z + ORDER[k] + NZ, rows), at_y(sign))

    def group(t, dy, zs=pl.ds(0, NZ), rows=pl.ds(0, ROWS)):
        yy = (y + dy + NY) % NY
        return gw.at[t, yy % 2, yy // 2, zs, core, rows]

    def upper(dz):
        return wblock(0, y, z + dz + NZ, UPPER)

    def lower(part):
        return lambda dz: gw.at[0, part, :, (z + dz + NZ) % NZ, core, LOWER]

    def far_send(key, ref_of, steps=(2, -2, 1, -1)):
        for dz in steps:
            zc[key, dz] = share(ref_of(0), at_z(dz))

    def far_relay(key, ref_of):
        far_wait(key, 2, -2)
        zc[key, 3] = share(ref_of(-2), at_z(1))
        zc[key, -3] = share(ref_of(2), at_z(-1))
        zc[key, 4] = share(ref_of(-2 * way), at_z(2 * way))

    def far_wait(key, *steps):
        for dz in steps:
            zc[key, dz].wait_recv()

    def y_send(*ks, t=0, rows=UPPER):
        for k in ks:
            y_send_one(k, t, rows)

    def y_relay(*ks, t=0, rows=UPPER):
        for k in ks:
            y_relay_one(k, t, rows)

    ALL = pl.ds(0, ROWS)

    def lower_to_sibling(*steps):
        for dz in steps:
            to_sibling("A", gw.at[0, :, :, (z + dz + NZ) % NZ, core, LOWER])

    def lower_send():
        for steps in ((2, -2), (1, -1)):
            for part in range(2):
                far_send(("lower", part), lower(part), steps)

    def lower_wait(*steps):
        for part in range(2):
            far_wait(("lower", part), *steps)

    def up_block(dz):
        return wblock(1, y, z + dz + NZ)

    def down_y_send():
        for dy in (1, -1, 2):
            yc["D", dy] = share(wblock(2, y, z), at_y(dy))

    def down_block(part):
        return lambda zz: gw.at[2, part, :, zz % NZ, core]

    def down_z(step):
        if step == 1:
            for dy in (1, -1, 2):
                yc["D", dy].wait_recv()
        for part in range(2):
            if step > 1:
                ring_wait(("D", part), step - 1)
            if step < 5:
                ring_send(("D", part), step, down_block(part))
        here = ((0,), (1, -1), (2, -2), (3, -3), (4,))[step - 1]
        for dz in here:
            to_sibling("D", plane(2, dz))

    def to_sibling(key, ref):
        dc.setdefault(key, []).append(share(ref, sibling))

    def sibling_wait(key):
        for copy in dc[key]:
            copy.wait_recv()

    def plane(t, dz, rows=pl.ds(0, ROWS)):
        return gw.at[t, :, :, (z + dz + NZ) % NZ, core, rows]

    rows_mine = pl.ds(pl.multiple_of(yl * PART, PART), PART)
    lanes_mine = pl.ds(pl.multiple_of(x * PIECE, 128), PIECE)
    ic = {}

    def input_send(g):
        for name, src, cg, device in (
            ("partner", blk.at[1 - yl, g, 1], 0, partner),
            ("both", blk.at[1 - yl, g, 0], 1, at_lon(-1, 1)),
            ("west", blk.at[yl, g, 0], 1, at_lon(-1, 0)),
        ):
            ic[g, name] = push(src, rin.at[g, cg, rows_mine], device)

    xc, xr = {}, {}

    def x_send(g):
        rin[g, 0, rows_mine] = blk[yl, g, 1]
        for name in ("partner", "both", "west"):
            ic[g, name].wait_recv()
        for cg in range(2):
            piece = rin[g, cg].astype(F32).T.reshape(4, 4, 8, PIECE)
            for w in range(4):
                part = piece[:, w].reshape(32, PIECE).astype(BF)
                xf[g, pl.ds(w * 64 + cg * 32, 32), lanes_mine] = part
        for half in range(2):
            for sign in (1, -1):
                rows = pl.ds((half if sign == 1 else 1 - half) * 128, 128)
                xc[g, sign, half] = share(xf.at[g, rows, lanes_mine], at_x(sign))

    def x_relay(g):
        for sign, half in ((1, 0), (-1, 1)):
            xc[g, sign, 0].wait_recv()
            lanes = pl.ds(pl.multiple_of(((x + 4 - sign) % NX) * PIECE, 128), PIECE)
            xr[g, sign] = share(xf.at[g, pl.ds(half * 128, 128), lanes], at_x(sign))

    def tables():
        k_of = lax.broadcasted_iota(jnp.int32, (15, 128), 1) // 8
        a_of = (
            lax.broadcasted_iota(jnp.int32, (8, 128), 1) % 8
            - lax.broadcasted_iota(jnp.int32, (8, 128), 0)
            + 7
        )
        for h in range(3):
            t = tb[h]
            wide = jnp.zeros((15, 128), F32)
            for b in range(15):
                wide = jnp.where(k_of == b, t[:, b:b + 1], wide)
            e = jnp.zeros((8, 128), F32)
            for a in range(15):
                e = jnp.where(a_of == a, wide[a:a + 1, :], e)
            ea[yl, h] = e
            ea[yl, 3 + h] = jnp.broadcast_to(sc[0:1, h:h + 1], (8, 128))
        copies = [share(ea.at[yl], partner)]
        here = lax.broadcasted_iota(jnp.int32, (1, PIECE), 1) // PART == yl
        rows = [
            jnp.where(here, jnp.concatenate([r[...], r[...]], axis=1), 0.0) for r in (rga, rgm)
        ]
        ga[yl, :, lanes_mine] = jnp.concatenate(rows + [jnp.zeros((6, PIECE), F32)], axis=0)
        ref = ga.at[yl, :, lanes_mine]
        return copies + [share(ref, peer(a, b)) for a, b in peers]

    row_j = lax.broadcasted_iota(jnp.int32, (64, 128), 0) % 8
    row_i = lax.broadcasted_iota(jnp.int32, (64, 128), 1) % 8
    poles = jnp.where((row_i >= 4) != (row_j >= 4), -1e9, 0.0).astype(F32)
    low = lax.broadcasted_iota(jnp.int32, (64, 128), 1) < 64
    low_bf = jnp.where(low, 1.0, 0.0).astype(BF)
    high_bf = jnp.where(low, 0.0, 1.0).astype(BF)
    HEADS_OF = [((0, 0), (0, 1)), ((1, 0), (1, 1)), ((0, 2), (1, 2))]

    def biases():
        for pair, members in enumerate(HEADS_OF):
            t0, t1 = (ea[part, h] for part, h in members)
            for cj in range(8):
                lo = (7 - cj) * 8
                bias[pair, pl.ds(cj * 8, 8), :] = jnp.concatenate(
                    [t0[:, lo:lo + 64], t1[:, lo:lo + 64]], axis=1
                )

    def unit(v):
        n = v.shape[1]
        same = (
            lax.broadcasted_iota(jnp.int32, (n, n), 0) // 64
            == lax.broadcasted_iota(jnp.int32, (n, n), 1) // 64
        )
        ones = jnp.where(same, 1.0, 0.0).astype(BF)
        square = v * v
        head = square.astype(BF)
        rest = (square - head.astype(F32)).astype(BF)
        total = nn(head, ones) + nn(rest, ones)
        return v * lax.rsqrt(total + 1e-6)

    def whole(g):
        for sign in (1, -1):
            xc[g, sign, 1].wait_recv()
            xr[g, sign].wait_recv()

    def qkv(g, part):
        w = gw[0, part, :, :, :, :, 0:640].reshape(D, 640)
        v = nn(xf[g], w).astype(BF).astype(F32)
        r = unit(v[:, :256])
        qn[g, part] = r[:, :128].astype(BF)
        kn[g, part] = r[:, 128:].astype(BF)
        vn[g, part] = v[:, 256:384].astype(BF)
        third[g, part, 0] = unit(v[:, 384:512])
        third[g, part, 1] = v[:, 512:]

    def third_pair(g):
        first = lax.broadcasted_iota(jnp.int32, (TOK, 128), 1) < 64
        (a0, v0), (a1, v1) = ((third[g, part, 0], third[g, part, 1]) for part in range(2))
        qn[g, 2] = jnp.where(first, a0, pltpu.roll(a1, 64, 1)).astype(BF)
        kn[g, 2] = jnp.where(first, pltpu.roll(a0, 64, 1), a1).astype(BF)
        vn[g, 2] = jnp.where(first, v0, pltpu.roll(v1, 64, 1)).astype(BF)

    def windows(g):
        def window(w):
            rows = pl.ds(w * 64, 64)
            for pair, ((p0, h0), (p1, h1)) in enumerate(HEADS_OF):
                qq = qn[g, pair, rows]
                both = jnp.concatenate([qq * low_bf, qq * high_bf], axis=0)
                s = nt(kn[g, pair, rows], both)
                scale = jnp.where(low[0:1], ea[p0, 3 + h0, 0:1, :], ea[p1, 3 + h1, 0:1, :])
                s = s * scale + bias[pair]
                if g == 1 and w == 3:
                    s = s + jnp.where(yl == 1, poles, 0.0)
                e = jnp.exp(s - jnp.max(s, axis=0, keepdims=True))
                e = e * (1.0 / jnp.sum(e, axis=0, keepdims=True))
                o = nn(e.astype(BF).T, vn[g, pair, rows])
                o = jnp.where(low, o[:64], o[64:])
                if pair < 2:
                    at[pair, rows, 128:256] = o.astype(BF)
                else:
                    at[0, rows, 0:128] = jnp.where(low, 0.0, pltpu.roll(o, 64, 1)).astype(BF)
                    at[1, rows, 0:128] = jnp.where(low, 0.0, o).astype(BF)

        for w in range(4):
            window(w)

    def x_rows(dx):
        return pl.ds(pl.multiple_of(((x + dx + NX) % NX) * 64, 64), 64)

    LEFT, RIGHT = pl.ds(0, 768), pl.ds(768, 768)
    pc = {}

    def proj(g):
        def columns(n):
            total = None
            for part in range(2):
                w = gw[0, part, n // 2, pl.ds((n % 2) * 4, 4), :, :, 512:768].reshape(PIECE, 256)
                term = nt(at[part], w)
                total = term if total is None else total + term
            pb[g, :, pl.ds(n * PIECE, PIECE)] = total.astype(BF)

        for n in range(4):
            columns(n)
        pc[g, "l", 1] = push(pb.at[g, x_rows(2), LEFT], rl.at[g, 0], at_x(1))
        pc[g, "l", -1] = push(pb.at[g, x_rows(2), RIGHT], rl.at[g, 1], at_x(-1))
        pc[g, "n", 1] = push(pb.at[g, x_rows(1), RIGHT], rp.at[g, 0, :, RIGHT], at_x(1))
        pc[g, "n", -1] = push(pb.at[g, x_rows(-1), LEFT], rp.at[g, 1, :, LEFT], at_x(-1))

    def proj_relay(g):
        for slot, (sign, lanes) in enumerate(((1, LEFT), (-1, RIGHT))):
            pc[g, "l", sign].wait_recv()
            rows = x_rows(sign)
            v = pb[g, rows, lanes].astype(F32) + rl[g, slot].astype(F32)
            pb[g, rows, lanes] = v.astype(BF)
            pc[g, "s", sign] = push(pb.at[g, rows, lanes], rp.at[g, slot, :, lanes], at_x(sign))

    ac, ar = {}, {}

    def norm_one(g):
        for what in ("n", "s"):
            for sign in (1, -1):
                pc[g, what, sign].wait_recv()
        v = pb[g, x_rows(0), :].astype(F32) + rp[g, 0].astype(F32) + rp[g, 1].astype(F32)
        mean = jnp.sum(v, axis=1, keepdims=True) * (1.0 / D)
        var = jnp.sum(v * v, axis=1, keepdims=True) * (1.0 / D) - mean * mean
        gains = ga[0, 0:1, :] + ga[1, 0:1, :]
        res = xf[g, x_rows(0), :].astype(F32)
        af[g, x_rows(0), :] = (res + (v - mean) * lax.rsqrt(var + 1e-5) * gains).astype(BF)
        for half in range(2):
            for sign in (1, -1):
                start = x * 64 + (half if sign == 1 else 1 - half) * 32
                ref = af.at[g, pl.ds(pl.multiple_of(start, 32), 32)]
                ac[g, sign, half] = share(ref, at_x(sign))

    def a_relay(g):
        for sign, half in ((1, 0), (-1, 1)):
            ac[g, sign, 0].wait_recv()
            start = ((x + 4 - sign) % NX) * 64 + half * 32
            ref = af.at[g, pl.ds(pl.multiple_of(start, 32), 32)]
            ar[g, sign] = share(ref, at_x(sign))

    def up(g):
        for sign in (1, -1):
            ac[g, sign, 1].wait_recv()
            ar[g, sign].wait_recv()

        def columns(n):
            w = gw[1, n // 3, :, :, :, :, pl.ds((n % 3) * 256, 256)].reshape(D, 256)
            hs[:, pl.ds(n * 256, 256)] = by_column(gelu(nn(af[g], w))).astype(BF)

        for n in range(6):
            columns(n)

    TOP, BOTTOM = pl.ds(0, PART), pl.ds(PART, PART)
    rc = {}

    def half(c):
        return pl.ds(c * 128, 128)

    def down(g):
        for slot, dx in ((0, 2), (1, 1), (2, 3), (3, 0)):
            xx = (x + dx) % NX
            total = None
            for part in range(2):
                w = gw[2, part, xx // 2, pl.ds((xx % 2) * 4, 4)].reshape(PIECE, PACK)
                term = nt(w, hs[:, part * PACK:part * PACK + PACK])
                total = term if total is None else total + term
            db[g, slot] = total.astype(BF)
            for c in range(2):
                if slot == 0:
                    for to, (sign, rows) in enumerate(((1, TOP), (-1, BOTTOM))):
                        rc[g, c, "l", sign] = push(
                            db.at[g, 0, rows, half(c)], rdl.at[g, to, :, half(c)], at_x(sign)
                        )
                elif slot < 3:
                    sign, rows = ((1, BOTTOM), (-1, TOP))[slot - 1]
                    rc[g, c, "n", sign] = push(
                        db.at[g, slot, rows, half(c)],
                        rd.at[g, slot - 1, rows, half(c)],
                        at_x(sign),
                    )

    def down_relay(g, c):
        for slot, (sign, rows) in enumerate(((1, TOP), (-1, BOTTOM))):
            rc[g, c, "l", sign].wait_recv()
            v = db[g, slot + 1, rows, half(c)].astype(F32)
            v = v + rdl[g, slot, :, half(c)].astype(F32)
            db[g, slot + 1, rows, half(c)] = v.astype(BF)
            rc[g, c, "s", sign] = push(
                db.at[g, slot + 1, rows, half(c)], rd.at[g, slot, rows, half(c)], at_x(sign)
            )

    tc = {}

    def stats(g, c):
        for what in ("n", "s"):
            for sign in (1, -1):
                rc[g, c, what, sign].wait_recv()
        v = db[g, 3, :, half(c)].astype(F32)
        v = v + rd[g, 0, :, half(c)].astype(F32) + rd[g, 1, :, half(c)].astype(F32)
        ss[g, c, 0:1, :] = jnp.sum(v, axis=0, keepdims=True)
        ss[g, c, 1:2, :] = jnp.sum(v * v, axis=0, keepdims=True)
        for slot, dx in ((0, 2), (1, 1), (2, 3)):
            tc[g, c, slot] = push(ss.at[g, c], st.at[g, c, slot], at_x(dx))
        return v

    oc = []

    def residual(g):
        res = by_column(af[g, :, lanes_mine].astype(F32)).T
        row = ga[0, 1:2, lanes_mine] + ga[1, 1:2, lanes_mine]
        return res, jnp.broadcast_to(row, (128, PIECE)).T

    def final(g, c, v, res, gains):
        for slot in range(3):
            tc[g, c, slot].wait_recv()
        tot = ss[g, c] + st[g, c, 0] + st[g, c, 1] + st[g, c, 2]
        mean = tot[0:1] * (1.0 / D)
        var = tot[1:2] * (1.0 / D) - mean * mean
        o = res[:, c * 128:c * 128 + 128] + (v - mean) * lax.rsqrt(var + 1e-5) * gains
        ob[g, c] = o.astype(BF).reshape(2, PART, 128)
        if c == 0:
            out[yl, g, 1] = ob[g, 0, yl]
            oc.append(push(ob.at[g, 0, 1 - yl], out.at[yl, g, 1], partner))
        else:
            oc.append(push(ob.at[g, 1, 1 - yl], out.at[yl, g, 0], at_lon(1, 1)))
            oc.append(push(ob.at[g, 1, yl], out.at[yl, g, 0], at_lon(1, 0)))

    far_send("upper", upper)
    for dy in (1, -1, 2):
        yc["first", dy] = share(wblock(0, y, z, LOWER), at_y(dy))
    input_send(0)
    y_send(0)
    ss[...] = jnp.zeros_like(ss)
    far_relay("upper", upper)
    for dy in (1, -1, 2):
        yc["first", dy].wait_recv()
    lower_send()
    input_send(1)
    far_wait("upper", 1, -1)
    y_send(1, 2, 3, 4)
    lower_to_sibling(0)
    x_send(0)
    far_wait("upper", 3, -3)
    y_send(5, 6)
    far_wait("upper", 4)
    y_send(7)
    y_relay(0)
    far_relay(("lower", 0), lower(0))
    far_relay(("lower", 1), lower(1))
    far_send("U", up_block)
    lower_to_sibling(2, -2)
    to_sibling("A", group(0, 0, rows=UPPER))
    x_relay(0)
    y_relay(1, 2, 3, 4)
    x_send(1)
    lower_wait(1, -1)
    lower_to_sibling(1, -1)
    y_relay(5, 6, 7)
    small = tables()
    down_y_send()
    y_send(0, t=1, rows=ALL)
    to_sibling("A", group(0, 1, rows=UPPER))
    to_sibling("A", group(0, -1, rows=UPPER))
    lower_wait(3, -3, 4)
    lower_to_sibling(3, -3, 4)
    x_relay(1)
    far_relay("U", up_block)
    for k in range(8):
        yr[0, k].wait_recv()
    to_sibling("B", group(0, 2, rows=UPPER))
    far_wait("U", 1, -1)
    y_send(1, 2, 3, 4, t=1, rows=ALL)
    sibling_wait("A")
    whole(0)
    qkv(0, 1 - yl)
    whole(1)
    qkv(1, 1 - yl)
    down_z(1)
    sibling_wait("B")
    qkv(0, yl)
    third_pair(0)
    for copy in small:
        copy.wait_recv()
    biases()
    far_wait("U", 3, -3, 4)
    y_send(5, 6, 7, t=1, rows=ALL)
    to_sibling("U", group(1, 0))
    windows(0)
    proj(0)
    qkv(1, yl)
    third_pair(1)
    windows(1)
    down_z(2)
    proj_relay(0)
    proj(1)
    y_relay(0, 1, 2, 3, 4, t=1, rows=ALL)
    norm_one(0)
    proj_relay(1)
    y_relay(5, 6, 7, t=1, rows=ALL)
    to_sibling("U", group(1, 1))
    to_sibling("U", group(1, -1))
    down_z(3)
    a_relay(0)
    for k in range(8):
        yr[1, k].wait_recv()
    to_sibling("U", group(1, 2))
    down_z(4)
    norm_one(1)
    sibling_wait("U")
    up(0)
    a_relay(1)
    down_z(5)
    sibling_wait("D")
    down(0)
    up(1)
    down_relay(0, 0)
    down_relay(0, 1)
    down(1)
    v0 = [stats(0, c) for c in range(2)]
    for c in range(2):
        down_relay(1, c)
    kept = residual(0)
    for c in range(2):
        final(0, c, v0[c], *kept)
    kept = residual(1)
    v1 = [stats(1, c) for c in range(2)]
    for c in range(2):
        final(1, c, v1[c], *kept)
    for cp in oc:
        cp.wait_recv()
    for cp in started:
        cp.wait_send()


def body(
    field, w_query, w_key, w_value, w_proj, w_up, w_down, logit_scale, rel_bias, gain_attn, gain_mlp
):
    anywhere = pl.BlockSpec(memory_space=pl.ANY)
    out = pl.pallas_call(
        kernel,
        out_shape=jax.ShapeDtypeStruct((2, 2, 2, PART, 128), BF),
        in_specs=[anywhere] * 11,
        out_specs=pl.BlockSpec(memory_space=pltpu.VMEM),
        scratch_shapes=[
            pltpu.VMEM((8, PART, 128), BF),
            pltpu.VMEM((ROWS, PART), BF),
            pltpu.VMEM((ROWS, PART), BF),
            pltpu.VMEM((ROWS, PART), BF),
            pltpu.VMEM((ROWS, PART), BF),
            pltpu.VMEM((1, 3), F32),
            pltpu.VMEM((3, 15, 15), F32),
            pltpu.VMEM((1, PART), F32),
            pltpu.VMEM((1, PART), F32),
            pltpu.VMEM((2, 2, 2, PART, 128), BF),
            pltpu.VMEM((3, 2, 2, NZ, 2, ROWS, PACK), BF),
            pltpu.VMEM((2, 2, PIECE, 128), BF),
            pltpu.VMEM((2, TOK, D), BF),
            pltpu.VMEM((2, 3, TOK, 128), BF),
            pltpu.VMEM((2, 3, TOK, 128), BF),
            pltpu.VMEM((2, 3, TOK, 128), BF),
            pltpu.VMEM((2, 2, 2, TOK, 128), F32),
            pltpu.VMEM((2, TOK, 256), BF),
            pltpu.VMEM((2, TOK, D), BF),
            pltpu.VMEM((2, 2, 64, 768), BF),
            pltpu.VMEM((2, 2, 64, D), BF),
            pltpu.VMEM((2, TOK, D), BF),
            pltpu.VMEM((TOK, D), BF),
            pltpu.VMEM((2, 4, PIECE, TOK), BF),
            pltpu.VMEM((2, 2, PART, TOK), BF),
            pltpu.VMEM((2, 2, PIECE, TOK), BF),
            pltpu.VMEM((2, 2, 8, 128), F32),
            pltpu.VMEM((2, 2, 3, 8, 128), F32),
            pltpu.VMEM((2, 8, D), F32),
            pltpu.VMEM((2, 8, 8, 128), F32),
            pltpu.VMEM((3, 64, 128), F32),
            pltpu.VMEM((2, 2, 2, PART, 128), BF),
            pltpu.SemaphoreType.DMA((11,)),
            pltpu.SemaphoreType.DMA((SEMS,)),
            pltpu.SemaphoreType.DMA((SEMS,)),
        ],
        compiler_params=pltpu.CompilerParams(
            collective_id=0, has_side_effects=True, vmem_limit_bytes=60 << 20
        ),
        name="block",
    )(
        field, w_query, w_key, w_value, w_proj.T, w_up, w_down.T,
        logit_scale.reshape(1, 3), rel_bias, gain_attn.reshape(1, PART), gain_mlp.reshape(1, PART),
    )
    mixed = out.reshape(2, 2, 2, PART, 4, 32).transpose(2, 4, 3, 0, 1, 5)
    return jnp.roll(mixed.reshape(8, PART, 128), 4, axis=2)


def solution(mesh):
    placed = (
        P("lon", "ch", None),
        P("lon", "ch"),
        P("lon", "ch"),
        P("lon", "ch"),
        P("ch", "lon"),
        P("lon", "ch"),
        P("ch", "lon"),
        P("ch"),
        P("ch", None, None),
        P("ch"),
        P("ch"),
    )
    return jax.shard_map(
        body, mesh=mesh, in_specs=placed, out_specs=P("lon", "ch", None), check_vma=False
    )
```

```python
import jax
import jax.numpy as jnp
from jax import lax
from jax.experimental import pallas as pl
from jax.experimental.pallas import tpu as pltpu
from jax.sharding import PartitionSpec as P

MESH = pl.DeviceIdType.MESH
BF = jnp.bfloat16
F32 = jnp.float32
D = 1536
NX, NY, NZ = 4, 4, 8
ROWS = 48
PACK = 768
TOK = 256
PART = 192
PIECE = 384
SEMS = 240


def nt(a, b):
    return lax.dot_general(a, b, (((1,), (1,)), ((), ())), preferred_element_type=F32)


def nn(a, b):
    return jnp.dot(a, b, preferred_element_type=F32)


def gelu(v):
    return 0.5 * v * (1.0 + lax.erf(v * 0.7071067811865476))


def by_column(v):
    v = v.reshape(4, 8, 8, v.shape[1])
    return jnp.concatenate([v[:, c].reshape(32, v.shape[3]) for c in range(8)], axis=0)


def kernel(
    field, w_query, w_key, w_value, w_proj, w_up, w_down, logit, rel, g_attn, g_mlp, out,
    fr, rq, rk, rv, rpj, sc, tb, rga, rgm,
    blk, gw, rin, xf, qn, kn, vn, third, at, pb, rl, rp, af, hs, db, rdl, rd, ss, st, ga, ea, bias, ob, oin,
    load, send, recv,
):
    lon = lax.axis_index("lon")
    ch = lax.axis_index("ch")
    x, yl = ch // 2, ch % 2
    core, z, yh = lon % 2, (lon // 2) % NZ, lon // (2 * NZ)
    y = yh * 2 + yl
    way = 1 - 2 * core

    def at_x(dx):
        return (lon, ((x + dx + NX) % NX) * 2 + yl)

    def at_z(dz):
        return ((yh * NZ + (z + dz + NZ) % NZ) * 2 + core, ch)

    def at_y(dy):
        yy = (y + dy + NY) % NY
        return (((yy // 2) * NZ + z) * 2 + core, x * 2 + yy % 2)

    sibling = (lon + 1 - 2 * core, ch)
    partner = (lon, x * 2 + 1 - yl)

    def at_lon(dl, other):
        c = x * 2 + 1 - yl if other else ch
        return ((lon + dl + 32) % 32, c)

    def peer(dx, other):
        c = 1 - yl if other else yl
        return (lon, ((x + dx) % NX) * 2 + c)

    peers = [(1, 0), (3, 0), (2, 0), (0, 1), (1, 1), (3, 1), (2, 1)]

    loads = []
    for src, dst in (
        (field, fr), (w_query, rq), (w_key, rk), (w_value, rv), (w_proj, rpj),
        (w_up, gw.at[1, yl, yh, z, core]), (w_down, gw.at[2, yl, yh, z, core]),
        (logit, sc), (rel, tb), (g_attn, rga), (g_mlp, rgm),
    ):
        copy = pltpu.make_async_copy(src, dst, load.at[len(loads)])
        copy.start()
        loads.append(copy)

    barrier = pltpu.get_barrier_semaphore()
    greeted = [peer(a, b) for a, b in peers]
    greeted += [at_z(dz) for dz in (1, -1, 2, -2, 3, -3, 4)]
    greeted += [at_y(1), at_y(-1), at_y(2), sibling]
    greeted += [at_lon(1, 0), at_lon(1, 1), at_lon(-1, 0), at_lon(-1, 1)]
    for device in greeted:
        pl.semaphore_signal(barrier, inc=1, device_id=device, device_id_type=MESH)

    for copy in loads:
        copy.wait()

    lane = lax.broadcasted_iota(jnp.int32, (32, 128), 1) // 32

    def regroup(i, carry):
        rows = pl.ds(pl.multiple_of(i * 32, 32), 32)
        for half in range(2):
            cols = [fr[half * 4 + j, rows, :].astype(F32) for j in range(4)]
            for k in range(4):
                v = None
                for j in range(4):
                    moved = pltpu.roll(cols[j], (32 * (j - k) - 4) % 128, 1)
                    v = moved if v is None else jnp.where(lane == j, moved, v)
                blk[k // 2, k % 2, half, rows, :] = v.astype(BF)
        return carry

    lax.fori_loop(0, PART // 32, regroup, 0)
    q, k, v = (r[...].astype(F32) for r in (rq, rk, rv))
    p = rpj[...].astype(F32)
    gw[0, yl, yh, z, core] = jnp.concatenate(
        [
            q[:, :128], k[:, :128], v[:, :128], q[:, 128:], k[:, 128:],
            v[:, 128:], p[:, 128:], p[:, :128],
        ],
        axis=1,
    ).astype(BF)

    pl.semaphore_wait(barrier, len(greeted))

    started = []

    def push(src, dst, device):
        i = len(started)
        copy = pltpu.make_async_remote_copy(
            src_ref=src, dst_ref=dst, send_sem=send.at[i], recv_sem=recv.at[i],
            device_id=device, device_id_type=MESH,
        )
        copy.start()
        started.append(copy)
        return copy

    def share(ref, device):
        return push(ref, ref, device)

    UPPER, LOWER = pl.ds(0, 32), pl.ds(32, 16)
    zc, yc, yr, dc = {}, {}, {}, {}

    def wblock(t, yy, zz, rows=pl.ds(0, ROWS)):
        return gw.at[t, yy % 2, yy // 2, zz % NZ, core, rows]

    def ring_send(key, s, ref_of):
        if s < 4:
            zc[key, s, 1] = share(ref_of(z - s + 1 + NZ), at_z(1))
            zc[key, s, -1] = share(ref_of(z + s - 1), at_z(-1))
        else:
            zc[key, s, 0] = share(ref_of(z - way * 3 + NZ), at_z(way))

    def ring_wait(key, s):
        for sign in (1, -1, 0):
            if (key, s, sign) in zc:
                zc[key, s, sign].wait_recv()

    ORDER = [0, 1, -1, 2, -2, 3, -3, 4]

    def y_send_one(k, t, rows):
        ref = wblock(t, y, z + ORDER[k] + NZ, rows)
        yc[t, k, 1] = share(ref, at_y(1))
        yc[t, k, -1] = share(ref, at_y(-1))

    def y_relay_one(k, t, rows):
        yc[t, k, 1].wait_recv()
        yc[t, k, -1].wait_recv()
        sign = 1 if k % 2 == 0 else -1
        yr[t, k] = share(wblock(t, (y - sign + NY) % NY, z + ORDER[k] + NZ, rows), at_y(sign))

    def group(t, dy, zs=pl.ds(0, NZ), rows=pl.ds(0, ROWS)):
        yy = (y + dy + NY) % NY
        return gw.at[t, yy % 2, yy // 2, zs, core, rows]

    def upper(dz):
        return wblock(0, y, z + dz + NZ, UPPER)

    def lower(part):
        return lambda dz: gw.at[0, part, :, (z + dz + NZ) % NZ, core, LOWER]

    def far_send(key, ref_of, steps=(2, -2, 1, -1)):
        for dz in steps:
            zc[key, dz] = share(ref_of(0), at_z(dz))

    def far_relay(key, ref_of):
        far_wait(key, 2, -2)
        zc[key, 3] = share(ref_of(-2), at_z(1))
        zc[key, -3] = share(ref_of(2), at_z(-1))
        zc[key, 4] = share(ref_of(-2 * way), at_z(2 * way))

    def far_wait(key, *steps):
        for dz in steps:
            zc[key, dz].wait_recv()

    def y_send(*ks, t=0, rows=UPPER):
        for k in ks:
            y_send_one(k, t, rows)

    def y_relay(*ks, t=0, rows=UPPER):
        for k in ks:
            y_relay_one(k, t, rows)

    ALL = pl.ds(0, ROWS)

    def lower_to_sibling(*steps):
        for dz in steps:
            to_sibling("A", gw.at[0, :, :, (z + dz + NZ) % NZ, core, LOWER])

    def lower_send():
        for steps in ((2, -2), (1, -1)):
            for part in range(2):
                far_send(("lower", part), lower(part), steps)

    def lower_wait(*steps):
        for part in range(2):
            far_wait(("lower", part), *steps)

    def up_block(dz):
        return wblock(1, y, z + dz + NZ)

    def down_y_send():
        for dy in (1, -1, 2):
            yc["D", dy] = share(wblock(2, y, z), at_y(dy))

    def down_block(part):
        return lambda zz: gw.at[2, part, :, zz % NZ, core]

    def down_z(step):
        if step == 1:
            for dy in (1, -1, 2):
                yc["D", dy].wait_recv()
        for part in range(2):
            if step > 1:
                ring_wait(("D", part), step - 1)
            if step < 5:
                ring_send(("D", part), step, down_block(part))
        here = ((0,), (1, -1), (2, -2), (3, -3), (4,))[step - 1]
        for dz in here:
            to_sibling("D", plane(2, dz))

    def to_sibling(key, ref):
        dc.setdefault(key, []).append(share(ref, sibling))

    def sibling_wait(key):
        for copy in dc[key]:
            copy.wait_recv()

    def plane(t, dz, rows=pl.ds(0, ROWS)):
        return gw.at[t, :, :, (z + dz + NZ) % NZ, core, rows]

    rows_mine = pl.ds(pl.multiple_of(yl * PART, PART), PART)
    lanes_mine = pl.ds(pl.multiple_of(x * PIECE, 128), PIECE)
    ic = {}

    def input_send(g):
        for name, src, cg, device in (
            ("partner", blk.at[1 - yl, g, 1], 0, partner),
            ("both", blk.at[1 - yl, g, 0], 1, at_lon(-1, 1)),
            ("west", blk.at[yl, g, 0], 1, at_lon(-1, 0)),
        ):
            ic[g, name] = push(src, rin.at[g, cg, rows_mine], device)

    xc, xr = {}, {}

    def x_send(g):
        rin[g, 0, rows_mine] = blk[yl, g, 1]
        for name in ("partner", "both", "west"):
            ic[g, name].wait_recv()
        for cg in range(2):
            piece = rin[g, cg].astype(F32).T.reshape(4, 4, 8, PIECE)
            for w in range(4):
                part = piece[:, w].reshape(32, PIECE).astype(BF)
                xf[g, pl.ds(w * 64 + cg * 32, 32), lanes_mine] = part
        for half in range(2):
            for sign in (1, -1):
                rows = pl.ds((half if sign == 1 else 1 - half) * 128, 128)
                xc[g, sign, half] = share(xf.at[g, rows, lanes_mine], at_x(sign))

    def x_relay(g):
        for sign, half in ((1, 0), (-1, 1)):
            xc[g, sign, 0].wait_recv()
            lanes = pl.ds(pl.multiple_of(((x + 4 - sign) % NX) * PIECE, 128), PIECE)
            xr[g, sign] = share(xf.at[g, pl.ds(half * 128, 128), lanes], at_x(sign))

    def tables():
        k_of = lax.broadcasted_iota(jnp.int32, (15, 128), 1) // 8
        a_of = (
            lax.broadcasted_iota(jnp.int32, (8, 128), 1) % 8
            - lax.broadcasted_iota(jnp.int32, (8, 128), 0)
            + 7
        )
        for h in range(3):
            t = tb[h]
            wide = jnp.zeros((15, 128), F32)
            for b in range(15):
                wide = jnp.where(k_of == b, t[:, b:b + 1], wide)
            e = jnp.zeros((8, 128), F32)
            for a in range(15):
                e = jnp.where(a_of == a, wide[a:a + 1, :], e)
            ea[yl, h] = e
            ea[yl, 3 + h] = jnp.broadcast_to(sc[0:1, h:h + 1], (8, 128))
        copies = [share(ea.at[yl], partner)]
        here = lax.broadcasted_iota(jnp.int32, (1, PIECE), 1) // PART == yl
        rows = [
            jnp.where(here, jnp.concatenate([r[...], r[...]], axis=1), 0.0) for r in (rga, rgm)
        ]
        ga[yl, :, lanes_mine] = jnp.concatenate(rows + [jnp.zeros((6, PIECE), F32)], axis=0)
        ref = ga.at[yl, :, lanes_mine]
        return copies + [share(ref, peer(a, b)) for a, b in peers]

    row_j = lax.broadcasted_iota(jnp.int32, (64, 128), 0) % 8
    row_i = lax.broadcasted_iota(jnp.int32, (64, 128), 1) % 8
    poles = jnp.where((row_i >= 4) != (row_j >= 4), -1e9, 0.0).astype(F32)
    low = lax.broadcasted_iota(jnp.int32, (64, 128), 1) < 64
    low_bf = jnp.where(low, 1.0, 0.0).astype(BF)
    high_bf = jnp.where(low, 0.0, 1.0).astype(BF)
    HEADS_OF = [((0, 0), (0, 1)), ((1, 0), (1, 1)), ((0, 2), (1, 2))]

    def biases():
        for pair, members in enumerate(HEADS_OF):
            t0, t1 = (ea[part, h] for part, h in members)
            for cj in range(8):
                lo = (7 - cj) * 8
                bias[pair, pl.ds(cj * 8, 8), :] = jnp.concatenate(
                    [t0[:, lo:lo + 64], t1[:, lo:lo + 64]], axis=1
                )

    def unit(v):
        n = v.shape[1]
        same = (
            lax.broadcasted_iota(jnp.int32, (n, n), 0) // 64
            == lax.broadcasted_iota(jnp.int32, (n, n), 1) // 64
        )
        ones = jnp.where(same, 1.0, 0.0).astype(BF)
        square = v * v
        head = square.astype(BF)
        rest = (square - head.astype(F32)).astype(BF)
        total = nn(head, ones) + nn(rest, ones)
        return v * lax.rsqrt(total + 1e-6)

    def whole(g):
        for sign in (1, -1):
            xc[g, sign, 1].wait_recv()
            xr[g, sign].wait_recv()

    def qkv(g, part):
        w = gw[0, part, :, :, :, :, 0:640].reshape(D, 640)
        v = nn(xf[g], w).astype(BF).astype(F32)
        r = unit(v[:, :256])
        qn[g, part] = r[:, :128].astype(BF)
        kn[g, part] = r[:, 128:].astype(BF)
        vn[g, part] = v[:, 256:384].astype(BF)
        third[g, part, 0] = unit(v[:, 384:512])
        third[g, part, 1] = v[:, 512:]

    def third_pair(g):
        first = lax.broadcasted_iota(jnp.int32, (TOK, 128), 1) < 64
        (a0, v0), (a1, v1) = ((third[g, part, 0], third[g, part, 1]) for part in range(2))
        qn[g, 2] = jnp.where(first, a0, pltpu.roll(a1, 64, 1)).astype(BF)
        kn[g, 2] = jnp.where(first, pltpu.roll(a0, 64, 1), a1).astype(BF)
        vn[g, 2] = jnp.where(first, v0, pltpu.roll(v1, 64, 1)).astype(BF)

    def windows(g):
        def window(w):
            rows = pl.ds(w * 64, 64)
            for pair, ((p0, h0), (p1, h1)) in enumerate(HEADS_OF):
                qq = qn[g, pair, rows]
                both = jnp.concatenate([qq * low_bf, qq * high_bf], axis=0)
                s = nt(kn[g, pair, rows], both)
                scale = jnp.where(low[0:1], ea[p0, 3 + h0, 0:1, :], ea[p1, 3 + h1, 0:1, :])
                s = s * scale + bias[pair]
                if g == 1 and w == 3:
                    s = s + jnp.where(yl == 1, poles, 0.0)
                e = jnp.exp(s - jnp.max(s, axis=0, keepdims=True))
                e = e * (1.0 / jnp.sum(e, axis=0, keepdims=True))
                o = nn(e.astype(BF).T, vn[g, pair, rows])
                o = jnp.where(low, o[:64], o[64:])
                if pair < 2:
                    at[pair, rows, 128:256] = o.astype(BF)
                else:
                    at[0, rows, 0:128] = jnp.where(low, 0.0, pltpu.roll(o, 64, 1)).astype(BF)
                    at[1, rows, 0:128] = jnp.where(low, 0.0, o).astype(BF)

        for w in range(4):
            window(w)

    def x_rows(dx):
        return pl.ds(pl.multiple_of(((x + dx + NX) % NX) * 64, 64), 64)

    LEFT, RIGHT = pl.ds(0, 768), pl.ds(768, 768)
    pc = {}

    def proj(g):
        def columns(n):
            total = None
            for part in range(2):
                w = gw[0, part, n // 2, pl.ds((n % 2) * 4, 4), :, :, 512:768].reshape(PIECE, 256)
                term = nt(at[part], w)
                total = term if total is None else total + term
            pb[g, :, pl.ds(n * PIECE, PIECE)] = total.astype(BF)

        for n in range(4):
            columns(n)
        pc[g, "l", 1] = push(pb.at[g, x_rows(2), LEFT], rl.at[g, 0], at_x(1))
        pc[g, "l", -1] = push(pb.at[g, x_rows(2), RIGHT], rl.at[g, 1], at_x(-1))
        pc[g, "n", 1] = push(pb.at[g, x_rows(1), RIGHT], rp.at[g, 0, :, RIGHT], at_x(1))
        pc[g, "n", -1] = push(pb.at[g, x_rows(-1), LEFT], rp.at[g, 1, :, LEFT], at_x(-1))

    def proj_relay(g):
        for slot, (sign, lanes) in enumerate(((1, LEFT), (-1, RIGHT))):
            pc[g, "l", sign].wait_recv()
            rows = x_rows(sign)
            v = pb[g, rows, lanes].astype(F32) + rl[g, slot].astype(F32)
            pb[g, rows, lanes] = v.astype(BF)
            pc[g, "s", sign] = push(pb.at[g, rows, lanes], rp.at[g, slot, :, lanes], at_x(sign))

    ac, ar = {}, {}

    def norm_one(g):
        for what in ("n", "s"):
            for sign in (1, -1):
                pc[g, what, sign].wait_recv()
        v = pb[g, x_rows(0), :].astype(F32) + rp[g, 0].astype(F32) + rp[g, 1].astype(F32)
        mean = jnp.sum(v, axis=1, keepdims=True) * (1.0 / D)
        var = jnp.sum(v * v, axis=1, keepdims=True) * (1.0 / D) - mean * mean
        gains = ga[0, 0:1, :] + ga[1, 0:1, :]
        res = xf[g, x_rows(0), :].astype(F32)
        af[g, x_rows(0), :] = (res + (v - mean) * lax.rsqrt(var + 1e-5) * gains).astype(BF)
        for half in range(2):
            for sign in (1, -1):
                start = x * 64 + (half if sign == 1 else 1 - half) * 32
                ref = af.at[g, pl.ds(pl.multiple_of(start, 32), 32)]
                ac[g, sign, half] = share(ref, at_x(sign))

    def a_relay(g):
        for sign, half in ((1, 0), (-1, 1)):
            ac[g, sign, 0].wait_recv()
            start = ((x + 4 - sign) % NX) * 64 + half * 32
            ref = af.at[g, pl.ds(pl.multiple_of(start, 32), 32)]
            ar[g, sign] = share(ref, at_x(sign))

    def up(g):
        for sign in (1, -1):
            ac[g, sign, 1].wait_recv()
            ar[g, sign].wait_recv()

        def columns(n):
            w = gw[1, n // 3, :, :, :, :, pl.ds((n % 3) * 256, 256)].reshape(D, 256)
            hs[:, pl.ds(n * 256, 256)] = by_column(gelu(nn(af[g], w))).astype(BF)

        for n in range(6):
            columns(n)

    TOP, BOTTOM = pl.ds(0, PART), pl.ds(PART, PART)
    rc = {}

    def half(c):
        return pl.ds(c * 128, 128)

    def down(g):
        for slot, dx in ((0, 2), (1, 1), (2, 3), (3, 0)):
            xx = (x + dx) % NX
            total = None
            for part in range(2):
                w = gw[2, part, xx // 2, pl.ds((xx % 2) * 4, 4)].reshape(PIECE, PACK)
                term = nt(w, hs[:, part * PACK:part * PACK + PACK])
                total = term if total is None else total + term
            db[g, slot] = total.astype(BF)
            for c in range(2):
                if slot == 0:
                    for to, (sign, rows) in enumerate(((1, TOP), (-1, BOTTOM))):
                        rc[g, c, "l", sign] = push(
                            db.at[g, 0, rows, half(c)], rdl.at[g, to, :, half(c)], at_x(sign)
                        )
                elif slot < 3:
                    sign, rows = ((1, BOTTOM), (-1, TOP))[slot - 1]
                    rc[g, c, "n", sign] = push(
                        db.at[g, slot, rows, half(c)],
                        rd.at[g, slot - 1, rows, half(c)],
                        at_x(sign),
                    )

    def down_relay(g, c):
        for slot, (sign, rows) in enumerate(((1, TOP), (-1, BOTTOM))):
            rc[g, c, "l", sign].wait_recv()
            v = db[g, slot + 1, rows, half(c)].astype(F32)
            v = v + rdl[g, slot, :, half(c)].astype(F32)
            db[g, slot + 1, rows, half(c)] = v.astype(BF)
            rc[g, c, "s", sign] = push(
                db.at[g, slot + 1, rows, half(c)], rd.at[g, slot, rows, half(c)], at_x(sign)
            )

    tc = {}

    def stats(g, c):
        for what in ("n", "s"):
            for sign in (1, -1):
                rc[g, c, what, sign].wait_recv()
        v = db[g, 3, :, half(c)].astype(F32)
        v = v + rd[g, 0, :, half(c)].astype(F32) + rd[g, 1, :, half(c)].astype(F32)
        ss[g, c, 0:1, :] = jnp.sum(v, axis=0, keepdims=True)
        ss[g, c, 1:2, :] = jnp.sum(v * v, axis=0, keepdims=True)
        for slot, dx in ((0, 2), (1, 1), (2, 3)):
            tc[g, c, slot] = push(ss.at[g, c], st.at[g, c, slot], at_x(dx))
        return v

    oc = []

    def residual(g):
        res = by_column(af[g, :, lanes_mine].astype(F32)).T
        row = ga[0, 1:2, lanes_mine] + ga[1, 1:2, lanes_mine]
        return res, jnp.broadcast_to(row, (128, PIECE)).T

    def final(g, c, v, res, gains):
        for slot in range(3):
            tc[g, c, slot].wait_recv()
        tot = ss[g, c] + st[g, c, 0] + st[g, c, 1] + st[g, c, 2]
        mean = tot[0:1] * (1.0 / D)
        var = tot[1:2] * (1.0 / D) - mean * mean
        o = res[:, c * 128:c * 128 + 128] + (v - mean) * lax.rsqrt(var + 1e-5) * gains
        ob[g, c] = o.astype(BF).reshape(2, PART, 128)
        if c == 0:
            oin[yl, g, 1] = ob[g, 0, yl]
            oc.append(push(ob.at[g, 0, 1 - yl], oin.at[yl, g, 1], partner))
        else:
            oc.append(push(ob.at[g, 1, 1 - yl], oin.at[yl, g, 0], at_lon(1, 1)))
            oc.append(push(ob.at[g, 1, yl], oin.at[yl, g, 0], at_lon(1, 0)))

    far_send("upper", upper)
    for dy in (1, -1, 2):
        yc["first", dy] = share(wblock(0, y, z, LOWER), at_y(dy))
    input_send(0)
    y_send(0)
    ss[...] = jnp.zeros_like(ss)
    far_relay("upper", upper)
    for dy in (1, -1, 2):
        yc["first", dy].wait_recv()
    lower_send()
    input_send(1)
    far_wait("upper", 1, -1)
    y_send(1, 2, 3, 4)
    lower_to_sibling(0)
    x_send(0)
    far_wait("upper", 3, -3)
    y_send(5, 6)
    far_wait("upper", 4)
    y_send(7)
    y_relay(0)
    far_relay(("lower", 0), lower(0))
    far_relay(("lower", 1), lower(1))
    far_send("U", up_block)
    lower_to_sibling(2, -2)
    to_sibling("A", group(0, 0, rows=UPPER))
    x_relay(0)
    y_relay(1, 2, 3, 4)
    x_send(1)
    lower_wait(1, -1)
    lower_to_sibling(1, -1)
    y_relay(5, 6, 7)
    small = tables()
    down_y_send()
    y_send(0, t=1, rows=ALL)
    to_sibling("A", group(0, 1, rows=UPPER))
    to_sibling("A", group(0, -1, rows=UPPER))
    lower_wait(3, -3, 4)
    lower_to_sibling(3, -3, 4)
    x_relay(1)
    far_relay("U", up_block)
    for k in range(8):
        yr[0, k].wait_recv()
    to_sibling("B", group(0, 2, rows=UPPER))
    far_wait("U", 1, -1)
    y_send(1, 2, 3, 4, t=1, rows=ALL)
    sibling_wait("A")
    whole(0)
    qkv(0, 1 - yl)
    whole(1)
    qkv(1, 1 - yl)
    down_z(1)
    sibling_wait("B")
    qkv(0, yl)
    third_pair(0)
    for copy in small:
        copy.wait_recv()
    biases()
    far_wait("U", 3, -3, 4)
    y_send(5, 6, 7, t=1, rows=ALL)
    to_sibling("U", group(1, 0))
    windows(0)
    proj(0)
    qkv(1, yl)
    third_pair(1)
    windows(1)
    down_z(2)
    proj_relay(0)
    proj(1)
    y_relay(0, 1, 2, 3, 4, t=1, rows=ALL)
    norm_one(0)
    proj_relay(1)
    y_relay(5, 6, 7, t=1, rows=ALL)
    to_sibling("U", group(1, 1))
    to_sibling("U", group(1, -1))
    down_z(3)
    a_relay(0)
    for k in range(8):
        yr[1, k].wait_recv()
    to_sibling("U", group(1, 2))
    down_z(4)
    norm_one(1)
    sibling_wait("U")
    up(0)
    a_relay(1)
    down_z(5)
    sibling_wait("D")
    down(0)
    up(1)
    down_relay(0, 0)
    down_relay(0, 1)
    down(1)
    v0 = [stats(0, c) for c in range(2)]
    for c in range(2):
        down_relay(1, c)
    kept = residual(0)
    for c in range(2):
        final(0, c, v0[c], *kept)
    kept = residual(1)
    v1 = [stats(1, c) for c in range(2)]
    for c in range(2):
        final(1, c, v1[c], *kept)
    for cp in oc:
        cp.wait_recv()

    quarter = (lax.broadcasted_iota(jnp.int32, (32, 128), 1) + 124) % 128 // 32

    def ungroup(i, carry):
        rows = pl.ds(pl.multiple_of(i * 32, 32), 32)
        for side in range(2):
            parts = [oin[k // 2, k % 2, side, rows, :].astype(F32) for k in range(4)]
            for j in range(4):
                v = None
                for k in range(4):
                    moved = pltpu.roll(parts[k], (32 * (k - j) + 4) % 128, 1)
                    v = moved if v is None else jnp.where(quarter == k, moved, v)
                out[side * 4 + j, rows, :] = v.astype(BF)
        return carry

    lax.fori_loop(0, PART // 32, ungroup, 0)
    for cp in started:
        cp.wait_send()


def body(
    field, w_query, w_key, w_value, w_proj, w_up, w_down, logit_scale, rel_bias, gain_attn, gain_mlp
):
    anywhere = pl.BlockSpec(memory_space=pl.ANY)
    return pl.pallas_call(
        kernel,
        out_shape=jax.ShapeDtypeStruct((8, PART, 128), BF),
        in_specs=[anywhere] * 11,
        out_specs=pl.BlockSpec(memory_space=pltpu.VMEM),
        scratch_shapes=[
            pltpu.VMEM((8, PART, 128), BF),
            pltpu.VMEM((ROWS, PART), BF),
            pltpu.VMEM((ROWS, PART), BF),
            pltpu.VMEM((ROWS, PART), BF),
            pltpu.VMEM((ROWS, PART), BF),
            pltpu.VMEM((1, 3), F32),
            pltpu.VMEM((3, 15, 15), F32),
            pltpu.VMEM((1, PART), F32),
            pltpu.VMEM((1, PART), F32),
            pltpu.VMEM((2, 2, 2, PART, 128), BF),
            pltpu.VMEM((3, 2, 2, NZ, 2, ROWS, PACK), BF),
            pltpu.VMEM((2, 2, PIECE, 128), BF),
            pltpu.VMEM((2, TOK, D), BF),
            pltpu.VMEM((2, 3, TOK, 128), BF),
            pltpu.VMEM((2, 3, TOK, 128), BF),
            pltpu.VMEM((2, 3, TOK, 128), BF),
            pltpu.VMEM((2, 2, 2, TOK, 128), F32),
            pltpu.VMEM((2, TOK, 256), BF),
            pltpu.VMEM((2, TOK, D), BF),
            pltpu.VMEM((2, 2, 64, 768), BF),
            pltpu.VMEM((2, 2, 64, D), BF),
            pltpu.VMEM((2, TOK, D), BF),
            pltpu.VMEM((TOK, D), BF),
            pltpu.VMEM((2, 4, PIECE, TOK), BF),
            pltpu.VMEM((2, 2, PART, TOK), BF),
            pltpu.VMEM((2, 2, PIECE, TOK), BF),
            pltpu.VMEM((2, 2, 8, 128), F32),
            pltpu.VMEM((2, 2, 3, 8, 128), F32),
            pltpu.VMEM((2, 8, D), F32),
            pltpu.VMEM((2, 8, 8, 128), F32),
            pltpu.VMEM((3, 64, 128), F32),
            pltpu.VMEM((2, 2, 2, PART, 128), BF),
            pltpu.VMEM((2, 2, 2, PART, 128), BF),
            pltpu.SemaphoreType.DMA((11,)),
            pltpu.SemaphoreType.DMA((SEMS,)),
            pltpu.SemaphoreType.DMA((SEMS,)),
        ],
        compiler_params=pltpu.CompilerParams(
            collective_id=0, has_side_effects=True, vmem_limit_bytes=60 << 20
        ),
        name="block",
    )(
        field, w_query, w_key, w_value, w_proj.T, w_up, w_down.T,
        logit_scale.reshape(1, 3), rel_bias, gain_attn.reshape(1, PART), gain_mlp.reshape(1, PART),
    )


def solution(mesh):
    placed = (
        P("lon", "ch", None),
        P("lon", "ch"),
        P("lon", "ch"),
        P("lon", "ch"),
        P("ch", "lon"),
        P("lon", "ch"),
        P("ch", "lon"),
        P("ch"),
        P("ch", None, None),
        P("ch"),
        P("ch"),
    )
    return jax.shard_map(
        body, mesh=mesh, in_specs=placed, out_specs=P("lon", "ch", None), check_vma=False
    )
```
